256 devices in a mesh: leaf: 64 (over z, x, core), lvl: 4 (over y).
Axes of the slice: x: 4, y: 4, z: 8, core: 2. Of those that a mesh axis runs over, the one named last changes fastest.
Arguments:
- charges: bfloat16 [1024, 256, 512], P('leaf', 'lvl'), may hold values from -6 to 6
- leaf_basis: bfloat16 [1024, 256, 64], P('leaf', 'lvl'), may hold values from -0.375 to 0.375
- near_blocks: bfloat16 [1024, 12, 256, 256], P('leaf', None, 'lvl'), may hold values from -0.109375 to 0.109375
- near_cols: int32 [1024, 12], P('leaf'), may hold values from 0 to 1023, as said below
- coupling_fine: float32 [1024, 4, 64, 64], P('leaf', 'lvl'), may hold values from -0.375 to 0.375
- coupling_middle: float32 [512, 4, 64, 64], P('leaf', 'lvl'), may hold values from -0.375 to 0.375
- coupling_coarse: float32 [256, 4, 64, 64], P('leaf', 'lvl'), may hold values from -0.375 to 0.375
- far_cols_fine: int32 [1024, 4], P('leaf', 'lvl'), may hold values from 0 to 1023, as said below
- far_cols_middle: int32 [512, 4], P('leaf', 'lvl'), may hold values from 0 to 511, as said below
- far_cols_coarse: int32 [256, 4], P('leaf', 'lvl'), may hold values from 0 to 255, as said below
- transfer_fine: float32 [1024, 64, 64], P('leaf'), may hold values from -0.5 to 0.5
- transfer_middle: float32 [512, 64, 64], P('leaf'), may hold values from -0.5 to 0.5
- transfer_coarse: float32 [256, 64, 64], P('leaf'), may hold values from -0.5 to 0.5
- top_coupling: float32 [128, 8, 64, 64], P('leaf', 'lvl'), may hold values from -0.25 to 0.25
- top_cols: int32 [128, 8], P('leaf', 'lvl'), may hold values from 0 to 127, as said below
Outputs:
- potentials: bfloat16 [1024, 256, 512], P('leaf', 'lvl')
The draws below stay inside these ranges and needn't reach their ends.
Inputs may be any that keep to these rules, and one draw needn't show every extreme that they name: `near_cols`: the clusters are ordered on a periodic line. The slots of row c hold, in some order, the 12 distinct clusters (c + d) mod 1024 for d from -6 to 5. `far_cols_fine`: the slots of row c hold, in some order, the 4 distinct clusters (c + d) mod 1024 with |d| from 7 to 8, none of them in the near field of c. `far_cols_middle`: the slots of row c hold, in some order, the 4 distinct clusters (c + d) mod (512) with |d| from 4 to 5, none holding a leaf in the near field of a leaf of c. `far_cols_coarse`: the slots of row c hold, in some order, the 4 distinct clusters (c + d) mod (256) with |d| from 3 to 4, none holding a leaf in the near field of a leaf of c. `top_cols`: the slots of row r hold 8 distinct roots, none of them r.
All inputs are finite; a program needn't handle non-finite values.
Results may differ from the reference program's by a relative error of at most 0.0065.
Values may be sent and summed in bfloat16 or wider, within the bound.
No kernel may reach another device: no remote copies, remote signals or barrier semaphores. Data moves between devices by JAX's collectives and lax.ppermute only.
A program may use at most 128 MiB of HBM per device.

```python
import jax
import jax.numpy as jnp
from jax import lax

LEAF_PTS = 256
BASIS_RANK = 64
VECTORS = 512
NEAR_SLOTS = 12
FAR_SLOTS = 4
TOP_SLOTS = 8
NEAR_REACH = 6
REACH_FINE = 8
REACH_MIDDLE = 5
REACH_COARSE = 4
LEAVES = 1024
ROOTS = 128


def shuffled_columns(key, count, offsets):
    width = offsets.shape[0]
    row_keys = jax.random.split(key, count)
    orders = jax.vmap(lambda one_key: jax.random.permutation(one_key, width))(row_keys)
    picked = jnp.take(offsets, orders)
    row_ids = jnp.arange(count, dtype=jnp.int32)[:, None]
    return jnp.mod(row_ids + picked, count).astype(jnp.int32)


def far_offsets(reach):
    half_count = FAR_SLOTS // 2
    lowest = reach - half_count + 1
    steps = lowest + jnp.arange(half_count, dtype=jnp.int32)
    return jnp.concatenate([-steps, steps]).astype(jnp.int32)


def draw_near_cols(key, part):
    key = jax.random.fold_in(key, 11)
    offsets = jnp.arange(NEAR_SLOTS, dtype=jnp.int32) - NEAR_REACH
    return shuffled_columns(key, LEAVES, offsets)


def draw_far_cols_fine(key, part):
    key = jax.random.fold_in(key, 23)
    return shuffled_columns(key, LEAVES, far_offsets(REACH_FINE))


def draw_far_cols_middle(key, part):
    key = jax.random.fold_in(key, 37)
    return shuffled_columns(key, LEAVES // 2, far_offsets(REACH_MIDDLE))


def draw_far_cols_coarse(key, part):
    key = jax.random.fold_in(key, 41)
    return shuffled_columns(key, LEAVES // 4, far_offsets(REACH_COARSE))


def draw_top_cols(key, part):
    key = jax.random.fold_in(key, 53)
    row_keys = jax.random.split(key, ROOTS)
    orders = jax.vmap(lambda one_key: jax.random.permutation(one_key, ROOTS - 1)[:TOP_SLOTS])(row_keys)
    row_ids = jnp.arange(ROOTS, dtype=jnp.int32)[:, None]
    return jnp.mod(row_ids + 1 + orders.astype(jnp.int32), ROOTS).astype(jnp.int32)


def block_scale(key, dims, pieces, smallest, high):
    loudness = 1.0
    for axis_at, parts in pieces:
        draws = jax.random.uniform(jax.random.fold_in(jax.random.fold_in(key, 6), axis_at), (parts,), jnp.float32, smallest / len(pieces), high / len(pieces))
        loudness = loudness * jnp.repeat(jnp.exp(draws), dims[axis_at] // parts).reshape((-1,) + (1,) * (len(dims) - 1 - axis_at))
    return loudness


def centred(rng, shape, scale, most, pieces=(), held_as=jnp.bfloat16):
    drawn = jax.random.normal(rng, shape, jnp.float32) * scale
    if len(pieces) > 0:
        drawn = block_scale(rng, shape, pieces, -0.22, 0.18) * drawn
    return jnp.clip(drawn, min=-most, max=most).astype(held_as)


def setup_inputs(seed: int = 0) -> dict:
    keys = jax.random.split(jax.random.key(seed), 16)
    charges = centred(keys[0], (LEAVES, LEAF_PTS, VECTORS), 1.0, 6.0, ((0, 64), (1, 4)))
    leaf_basis = centred(keys[1], (LEAVES, LEAF_PTS, BASIS_RANK), LEAF_PTS ** -0.5, 0.375, ((0, 64), (1, 4)))
    near_blocks = centred(keys[2], (LEAVES, NEAR_SLOTS, LEAF_PTS, LEAF_PTS), (NEAR_SLOTS * LEAF_PTS) ** -0.5, 0.109375, ((0, 64), (2, 4)))
    near_cols = draw_near_cols(jax.random.fold_in(keys[15], 71), 0)
    coupling_fine = centred(keys[4], (LEAVES, FAR_SLOTS, BASIS_RANK, BASIS_RANK), (FAR_SLOTS * BASIS_RANK) ** -0.5, 0.375, ((0, 64), (1, 4)), jnp.float32)
    coupling_middle = centred(keys[5], (LEAVES // 2, FAR_SLOTS, BASIS_RANK, BASIS_RANK), (FAR_SLOTS * BASIS_RANK) ** -0.5, 0.375, ((0, 64), (1, 4)), jnp.float32)
    coupling_coarse = centred(keys[6], (LEAVES // 4, FAR_SLOTS, BASIS_RANK, BASIS_RANK), (FAR_SLOTS * BASIS_RANK) ** -0.5, 0.375, ((0, 64), (1, 4)), jnp.float32)
    far_cols_fine = draw_far_cols_fine(jax.random.fold_in(keys[15], 71), 0)
    far_cols_middle = draw_far_cols_middle(jax.random.fold_in(keys[15], 71), 0)
    far_cols_coarse = draw_far_cols_coarse(jax.random.fold_in(keys[15], 71), 0)
    transfer_fine = centred(keys[10], (LEAVES, BASIS_RANK, BASIS_RANK), (2 * BASIS_RANK) ** -0.5, 0.5, ((0, 64),), jnp.float32)
    transfer_middle = centred(keys[11], (LEAVES // 2, BASIS_RANK, BASIS_RANK), (2 * BASIS_RANK) ** -0.5, 0.5, ((0, 64),), jnp.float32)
    transfer_coarse = centred(keys[12], (LEAVES // 4, BASIS_RANK, BASIS_RANK), (2 * BASIS_RANK) ** -0.5, 0.5, ((0, 64),), jnp.float32)
    top_coupling = centred(keys[13], (ROOTS, TOP_SLOTS, BASIS_RANK, BASIS_RANK), (TOP_SLOTS * BASIS_RANK) ** -0.5, 0.25, ((0, 64), (1, 4)), jnp.float32)
    top_cols = draw_top_cols(jax.random.fold_in(keys[15], 71), 0)
    return {"charges": charges, "leaf_basis": leaf_basis, "near_blocks": near_blocks, "near_cols": near_cols, "coupling_fine": coupling_fine, "coupling_middle": coupling_middle, "coupling_coarse": coupling_coarse, "far_cols_fine": far_cols_fine, "far_cols_middle": far_cols_middle, "far_cols_coarse": far_cols_coarse, "transfer_fine": transfer_fine, "transfer_middle": transfer_middle, "transfer_coarse": transfer_coarse, "top_coupling": top_coupling, "top_cols": top_cols}


def lifted_moments(moments, transfer):
    lifted = jnp.einsum("cak,car->ckr", transfer, moments, precision=lax.Precision.HIGHEST)
    return lifted.reshape(lifted.shape[0] // 2, 2, lifted.shape[1], lifted.shape[2]).sum(axis=1)


def lowered_local(parent_local, transfer, coupled):
    spread = jnp.repeat(parent_local, 2, axis=0)
    return coupled + jnp.einsum("cak,ckr->car", transfer, spread, precision=lax.Precision.HIGHEST)


def coupled_terms(sources, blocks, columns):
    total = jnp.zeros((columns.shape[0],) + sources.shape[1:], jnp.float32)
    for slot_at in range(columns.shape[1]):
        picked = jnp.take(sources, columns[:, slot_at], axis=0)
        total = total + jnp.einsum("cab,cbr->car", blocks[:, slot_at], picked, precision=lax.Precision.HIGHEST)
    return total


def reference(charges, leaf_basis, near_blocks, near_cols, coupling_fine, coupling_middle, coupling_coarse, far_cols_fine, far_cols_middle, far_cols_coarse, transfer_fine, transfer_middle, transfer_coarse, top_coupling, top_cols):
    def near_slot(slot_at, total):
        picked = jnp.take(charges, near_cols[:, slot_at], axis=0).astype(jnp.float32)
        block = near_blocks[:, slot_at].astype(jnp.float32)
        return total + jnp.einsum("cpq,cqr->cpr", block, picked)

    near_field = lax.fori_loop(0, NEAR_SLOTS, near_slot, jnp.zeros(charges.shape, jnp.float32))
    basis_wide = leaf_basis.astype(jnp.float32)
    moments_fine = jnp.einsum("cpk,cpr->ckr", basis_wide, charges.astype(jnp.float32))
    moments_middle = lifted_moments(moments_fine, transfer_fine)
    moments_coarse = lifted_moments(moments_middle, transfer_middle)
    moments_root = lifted_moments(moments_coarse, transfer_coarse)
    term_fine = coupled_terms(moments_fine, coupling_fine, far_cols_fine)
    term_middle = coupled_terms(moments_middle, coupling_middle, far_cols_middle)
    term_coarse = coupled_terms(moments_coarse, coupling_coarse, far_cols_coarse)
    term_top = coupled_terms(moments_root, top_coupling, top_cols)
    local_coarse = lowered_local(term_top, transfer_coarse, term_coarse)
    local_middle = lowered_local(local_coarse, transfer_middle, term_middle)
    local_fine = lowered_local(local_middle, transfer_fine, term_fine)
    leaf_local = local_fine.astype(jnp.bfloat16).astype(jnp.float32)
    far_field = jnp.einsum("cpk,ckr->cpr", basis_wide, leaf_local)
    return (near_field + far_field).astype(jnp.bfloat16)
```

```python
import jax
import jax.numpy as jnp
from jax import lax
from jax.experimental import pallas as pl
from jax.experimental.pallas import tpu as pltpu
from jax.sharding import PartitionSpec as P

MIB = 1 << 20
BF = jnp.bfloat16
F32 = jnp.float32
ZS, XS, CS, LV = 8, 4, 2, 4
LEAVES, POINTS, VECTORS, RANK = 16, 64, 512, 64
PART = VECTORS // LV
LOW, HIGH = 6, 5
RELATIVE = (0, -1, 1, 2)


def shape(dims, dtype=BF):
    return jax.ShapeDtypeStruct(dims, dtype)


def mm(a, b):
    return jnp.dot(a, b, preferred_element_type=F32)


def leaf_pairs(dz=0, dx=0, dcore=0, step=0):
    pairs = []
    for at in range(ZS * XS * CS):
        z, x, core = at // (XS * CS), at // CS % XS, at % CS
        to = (((z + dz) % ZS) * XS + (x + dx) % XS) * CS + (core + dcore) % CS
        pairs.append((at, (to + step) % (ZS * XS * CS)))
    return pairs


def over_leaf(array, **move):
    return lax.ppermute(array, "leaf", leaf_pairs(**move))


def over_lvl(array, step):
    return lax.ppermute(array, "lvl", [(i, (i + step) % LV) for i in range(LV)])


SMEM = pl.BlockSpec(memory_space=pltpu.SMEM)
ANY = pl.BlockSpec(memory_space=pl.ANY)
HBM = pl.BlockSpec(memory_space=pltpu.HBM)


def after(array, *others):
    return lax.optimization_barrier((array,) + others)[0]


def kernel_call(kernel, scalars, arrays, outs, scratch=(), copies=32, limit=16, given=(), flops=10**6):
    return pl.pallas_call(
        kernel,
        out_shape=outs,
        in_specs=[SMEM] * len(scalars) + [ANY] * len(arrays) + [HBM] * len(given),
        out_specs=jax.tree.map(lambda _: ANY, outs),
        scratch_shapes=list(scratch) + [pltpu.SemaphoreType.DMA((copies,))],
        cost_estimate=pl.CostEstimate(flops=flops, bytes_accessed=10**5, transcendentals=0),
        compiler_params=pltpu.CompilerParams(vmem_limit_bytes=limit * MIB),
    )(*scalars, *arrays, *given)


class Copies:
    def __init__(self, sems):
        self.sems, self.count = sems, 0

    def start(self, source, target):
        copy = pltpu.make_async_copy(source, target, self.sems.at[self.count])
        self.count += 1
        copy.start()
        return copy


    def either(self, first, sources, target):
        at = self.sems.at[self.count]
        self.count += 1
        pl.when(first)(lambda: pltpu.make_async_copy(sources[0], target, at).start())
        pl.when(jnp.logical_not(first))(lambda: pltpu.make_async_copy(sources[1], target, at).start())
        return pltpu.make_async_copy(sources[0], target, at)


def lanes_of(k):
    return slice(RANK * (k % 8), RANK * (k % 8 + 1))


def own_core():
    return lax.rem(lax.axis_index("leaf"), CS)


def lvl_at(k):
    return lax.rem(lax.axis_index("lvl") + RELATIVE[k] + LV, LV)


def lifted(transfer, moments, count):
    parents = []
    for q in range(count // 2):
        both = transfer[2 * q : 2 * q + 2].reshape(2 * RANK, RANK).astype(BF).T
        parents.append(mm(both, jnp.concatenate(moments[2 * q : 2 * q + 2], axis=0)).astype(BF))
    return parents


def pack_kernel(
    charges, basis, fine_c, middle_c, coarse_c, top_c, edge, inner,
    v_edge, v_inner, v_basis, v_fine, v_middle, v_coarse, v_top, sems,
):
    copies = Copies(sems)
    edges = [
        copies.start(charges.at[pl.ds(0, 5)], v_edge.at[pl.ds(0, 5)]),
        copies.start(charges.at[pl.ds(10, 6)], v_edge.at[pl.ds(5, 6)]),
    ]
    loads = [copies.start(basis, v_basis), copies.start(charges.at[pl.ds(5, 5)], v_inner.at[pl.ds(0, 5)])]
    loads += [copies.start(a, b) for a, b in ((fine_c, v_fine), (middle_c, v_middle), (coarse_c, v_coarse), (top_c, v_top))]
    for load in edges:
        load.wait()
    out = [copies.start(v_edge, edge)]
    for load in loads:
        load.wait()
    for c in range(LEAVES):
        v_inner[5 + c // 8, :, lanes_of(c)] = v_basis[c].T
    blocks = [v_fine[c, 0] for c in range(16)] + [v_middle[c, 0] for c in range(8)]
    blocks += [v_coarse[c, 0] for c in range(4)] + [v_top[i, s] for i in range(2) for s in range(2)]
    for at, block in enumerate(blocks):
        v_inner[7 + at // 8, :, lanes_of(at)] = block.astype(BF)
    out.append(copies.start(v_inner, inner))
    for copy in out:
        copy.wait()


def leaf_of(edge, inner, c):
    if c < 5:
        return edge[c]
    return inner[c - 5] if c < 10 else edge[c - 5]


def basis_of(inner, c):
    return inner[5 + c // 8, :, lanes_of(c)]


def root_kernel(
    fine_cols, middle_cols, coarse_cols, top_cols, edge, inner, fine_t, middle_t, coarse_t,
    part0, part1, part2, part3, v_edge, v_inner, v_fine, v_middle, v_coarse, roots, sems,
):
    copies = Copies(sems)
    loads = [
        copies.start(a, b)
        for a, b in ((edge, v_edge), (inner.at[pl.ds(0, 7)], v_inner), (fine_t, v_fine), (middle_t, v_middle), (coarse_t, v_coarse))
    ]
    lane = lax.broadcasted_iota(jnp.int32, (16, PART), 1)
    info = jnp.zeros((16, PART), F32)
    leaf = lax.axis_index("leaf")
    at = 0
    for cols, count, total in ((fine_cols, 16, 1024), (middle_cols, 8, 512), (coarse_cols, 4, 256)):
        for c in range(count):
            away = ((cols[c] - leaf * count - c + total // 2) & (total - 1)) - total // 2
            info = jnp.where(lane == at, away.astype(F32), info)
            at += 1
    for i in range(2):
        for s in range(2):
            info = jnp.where(lane == at, top_cols[i, s].astype(F32), info)
            at += 1
    for load in loads:
        load.wait()
    moments = []
    for c in range(LEAVES):
        moments.append(mm(basis_of(v_inner, c), leaf_of(v_edge, v_inner, c)).astype(BF))
    moments = lifted(v_fine, moments, 16)
    moments = lifted(v_middle, moments, 8)
    moments = lifted(v_coarse, moments, 4)
    for j in range(LV):
        for i in range(2):
            roots[j, RANK * i : RANK * (i + 1)] = moments[i][:, PART * j : PART * (j + 1)]
        roots[j, 128:144] = info.astype(BF)
    out = [
        copies.start(roots.at[lax.rem(lax.axis_index("lvl") + k, LV)], part)
        for k, part in enumerate((part0, part1, part2, part3))
    ]
    for copy in out:
        copy.wait()


def read_columns(copies, parts, v_parts, v_cols, s_cols, columns):
    for load in [copies.start(part.at[pl.ds(128, 16)], v_parts.at[k]) for k, part in enumerate(parts)]:
        load.wait()
    for k in range(LV):
        v_cols[k] = v_parts[k].astype(F32)[0:8].astype(jnp.int32)
    copies.start(v_cols, s_cols).wait()
    return copies.start(v_cols, columns)


def columns_scratch():
    return [
        pltpu.VMEM((LV, 16, PART), BF), pltpu.VMEM((LV, 8, PART), jnp.int32), pltpu.SMEM((LV, 8, PART), jnp.int32),
    ]


def moments_kernel(
    edge0, inner0, edge1, inner1, edge2, inner2, edge3, inner3, fine_t, middle_t,
    fine_m, middle_m, coarse_m, to_right, to_left, edges, inners, v_fine, v_middle, moments, sems,
):
    copies = Copies(sems)
    loads = [copies.start(a, edges.at[k]) for k, a in enumerate((edge0, edge1, edge2, edge3))]
    loads += [copies.start(a.at[pl.ds(0, 7)], inners.at[k]) for k, a in enumerate((inner0, inner1, inner2, inner3))]
    loads += [copies.start(fine_t, v_fine), copies.start(middle_t, v_middle)]
    for load in loads:
        load.wait()
    fine = []
    for c in range(LEAVES):
        turned = [basis_of(inners.at[k], c) for k in range(LV)]
        points = [leaf_of(edges.at[k], inners.at[k], c) for k in range(LV)]
        fine.append(mm(jnp.concatenate(turned, axis=1), jnp.concatenate(points, axis=0)).astype(BF))
        moments[c] = fine[c]
    out = [
        copies.start(moments.at[pl.ds(8, 8)], to_right.at[pl.ds(0, 8)]),
        copies.start(moments.at[pl.ds(0, 8)], to_left.at[pl.ds(0, 8)]),
        copies.start(moments.at[pl.ds(0, 16)], fine_m),
    ]
    middle = lifted(v_fine, fine, 16)
    for c in range(8):
        moments[16 + c] = middle[c]
    out += [
        copies.start(moments.at[pl.ds(19, 5)], to_right.at[pl.ds(8, 5)]),
        copies.start(moments.at[pl.ds(16, 5)], to_left.at[pl.ds(8, 5)]),
        copies.start(moments.at[pl.ds(16, 8)], middle_m),
    ]
    coarse = lifted(v_middle, middle, 8)
    for c in range(4):
        moments[24 + c] = coarse[c]
    out += [copies.start(moments.at[pl.ds(24, 4)], to.at[pl.ds(13, 4)]) for to in (to_right, to_left)]
    out.append(copies.start(moments.at[pl.ds(24, 4)], coarse_m))
    for copy in out:
        copy.wait()


def ends_kernel(edge0, edge1, edge2, edge3, to_core, to_chip, v_core, v_chip, sems):
    copies = Copies(sems)
    core = own_core()
    loads = []
    for k, edge in enumerate((edge0, edge1, edge2, edge3)):
        loads.append(copies.start(edge.at[pl.ds(HIGH - HIGH * core, LOW)], v_core.at[pl.ds(LOW * k, LOW)]))
        loads.append(copies.start(edge.at[pl.ds(HIGH * core, LOW)], v_chip.at[pl.ds(LOW * k, LOW)]))
    for load in loads:
        load.wait()
    out = [copies.start(v_chip, to_chip), copies.start(v_core, to_core)]
    for copy in out:
        copy.wait()


def core_swap(array):
    return over_leaf(array, dcore=1)


def chip_swap(array):
    leaves = ZS * XS * CS
    return lax.ppermute(array, "leaf", [(i, (i + (1 if i % CS else -1)) % leaves) for i in range(leaves)])


def joined_kernel(*refs):
    copies = Copies(refs[-1])
    held, target, loads, out, at = refs[-2], refs[-3], [], [], 0
    for piece in refs[:-3]:
        loads.append((at, piece.shape[0], copies.start(piece, held.at[pl.ds(at, piece.shape[0])])))
        at += piece.shape[0]
    for at, count, load in loads:
        load.wait()
        out.append(copies.start(held.at[pl.ds(at, count)], target.at[pl.ds(at, count)]))
    for copy in out:
        copy.wait()


def joined(*pieces, flops=10**6):
    dims = (sum(piece.shape[0] for piece in pieces),) + pieces[0].shape[1:]
    return kernel_call(joined_kernel, (), pieces, shape(dims), scratch=[pltpu.VMEM(dims, BF)], flops=flops)


def near_kernel(
    near_cols, edge0, inner0, edge1, inner1, edge2, inner2, edge3, inner3, core_ends, chip_ends,
    blocks, out, points, held, total, slots, sems,
):
    copies = Copies(sems)
    block_copies = [copies.start(blocks.at[pl.ds(0, 4)], held.at[pl.ds(0, 4)])]
    even = own_core() == 0
    loads = []
    for k, (edge, inner) in enumerate(((edge0, inner0), (edge1, inner1), (edge2, inner2), (edge3, inner3))):
        row = pl.ds(pl.multiple_of(lvl_at(k) * POINTS, POINTS), POINTS)
        for source, first, count, leaf in ((edge, 0, 5, LOW), (inner, 0, 5, LOW + 5), (edge, 5, 6, LOW + 10)):
            loads.append(copies.start(source.at[pl.ds(first, count)], points.at[pl.ds(leaf, count), row, :]))
        core, chip = (end.at[pl.ds(LOW * k, LOW)] for end in (core_ends, chip_ends))
        loads.append(copies.either(even, (chip, core), points.at[pl.ds(0, LOW), row, :]))
        core, chip = (end.at[pl.ds(LOW * k, HIGH)] for end in (core_ends, chip_ends))
        loads.append(copies.either(even, (core, chip), points.at[pl.ds(LOW + 16, HIGH), row, :]))
    for g in range(1, 4):
        block_copies.append(copies.start(blocks.at[pl.ds(4 * g, 4)], held.at[pl.ds(4 * g, 4)]))
    first_leaf = lax.axis_index("leaf") * LEAVES

    def place_slots(c, carry):
        for s in range(12):
            slots[c, (near_cols[c, s] - first_leaf - c + LOW) & 1023] = s
        return carry

    lax.fori_loop(0, LEAVES, place_slots, 0)
    for load in loads:
        load.wait()
    stores = []
    for g in range(4):
        block_copies[g].wait()
        for source in range(15):
            held_by = [c for c in range(4) if 0 <= source - c < 12]
            rows = jnp.concatenate([held[4 * g + c, slots[4 * g + c, source - c]] for c in held_by], axis=0)
            product = mm(rows, points[4 * g + source])
            for i, c in enumerate(held_by):
                piece = product[POINTS * i : POINTS * (i + 1)]
                total[4 * g + c] = piece if source == c else total[4 * g + c] + piece
        stores.append(copies.start(total.at[pl.ds(4 * g, 4)], out.at[pl.ds(4 * g, 4)]))
    for store in stores:
        store.wait()


def top_kernel(
    part0, part1, part2, part3, own, up, down, far, mine, partner, out, columns,
    v_parts, v_cols, s_cols, v_couplings, sources, result, sems,
):
    copies = Copies(sems)
    loads = [
        copies.start(piece.at[pl.ds(10, 1), :, pl.ds(256, 256)], v_couplings.at[pl.ds(k, 1)])
        for k, piece in enumerate((own, up, down, far))
    ]
    store = read_columns(copies, (part0, part1, part2, part3), v_parts, v_cols, s_cols, columns)
    leaf = lax.axis_index("leaf")
    for k in range(LV):
        for j in range(4):
            root = s_cols[k, 0, 28 + j]
            there = root // 2
            hop = lax.rem(there // CS % XS - leaf // CS % XS + XS, XS)
            hop = jnp.where(hop == 3, 1, jnp.where(hop == 1, 2, jnp.where(hop == 2, 3, 0)))
            up_z = lax.rem(there // (XS * CS) - leaf // (XS * CS) + 4 + ZS, ZS)
            spot = hop * 16 + up_z * 2 + lax.rem(root, 2)
            here = lax.rem(there, CS) == lax.rem(leaf, CS)
            target = sources.at[(j // 2) * 8 + k * 2 + j % 2]
            loads.append(copies.either(here, (mine.at[spot], partner.at[spot]), target))
    for load in loads:
        load.wait()
    for i in range(2):
        lhs = jnp.concatenate([v_couplings[k, :, 128 * i : 128 * (i + 1)] for k in range(LV)], axis=1)
        rhs = jnp.concatenate([sources[8 * i + n] for n in range(8)], axis=0)
        result[i] = mm(lhs, rhs).astype(BF)
    copies.start(result, out).wait()
    store.wait()


def last_kernel(
    s_cols, fine_m, middle_m, coarse_m, low, high, inner0, inner1, inner2, inner3,
    own_t, up_t, down_t, far_t, near, fine_t, middle_t, coarse_t, basis, out,
    wide, v_couplings, top, v_fine, v_middle, v_coarse, v_basis, v_near, v_out, sems,
):
    copies = Copies(sems)
    early = []
    for k, inner in enumerate((inner0, inner1, inner2, inner3)):
        early.append(copies.start(inner.at[pl.ds(7, 4)], v_couplings.at[k]))
    early += [
        copies.start(coarse_t, v_coarse), copies.start(low.at[pl.ds(13, 4)], wide.at[pl.ds(0, 4)]),
        copies.start(coarse_m, wide.at[pl.ds(4, 4)]), copies.start(high.at[pl.ds(13, 4)], wide.at[pl.ds(8, 4)]),
    ]
    for k, piece in enumerate((own_t, up_t, down_t, far_t)):
        early.append(copies.start(piece, top.at[lvl_at(k)]))
    early_middle = [
        copies.start(middle_t, v_middle), copies.start(low.at[pl.ds(8, 5)], wide.at[pl.ds(12, 5)]),
        copies.start(middle_m, wide.at[pl.ds(17, 8)]), copies.start(high.at[pl.ds(8, 5)], wide.at[pl.ds(25, 5)]),
    ]
    early_fine = [
        copies.start(fine_t, v_fine), copies.start(basis, v_basis), copies.start(low.at[pl.ds(0, 8)], wide.at[pl.ds(30, 8)]),
        copies.start(fine_m, wide.at[pl.ds(38, 16)]), copies.start(high.at[pl.ds(0, 8)], wide.at[pl.ds(54, 8)]),
    ]
    near_loads = [copies.start(near.at[pl.ds(4 * g, 4)], v_near.at[pl.ds(4 * g, 4)]) for g in range(4)]

    def term(place, c, at):
        lhs = jnp.concatenate([v_couplings[k, at // 8, :, lanes_of(at)] for k in range(LV)], axis=1)
        return mm(lhs, jnp.concatenate([wide[place + c + s_cols[k, at]] for k in range(LV)], axis=0))

    for load in early:
        load.wait()
    coarse = []
    for c in range(4):
        parent = jnp.concatenate([top[j, c // 2] for j in range(LV)], axis=1)
        coarse.append((term(4, c, 24 + c) + mm(v_coarse[c].astype(BF), parent)).astype(BF))
    for load in early_middle:
        load.wait()
    middle = [
        (term(17, c, 16 + c) + mm(v_middle[c].astype(BF), coarse[c // 2])).astype(BF) for c in range(8)
    ]
    for load in early_fine:
        load.wait()
    stores = []
    for c in range(16):
        if c % 4 == 0:
            near_loads[c // 4].wait()
        local = term(38, c, c) + mm(v_fine[c].astype(BF), middle[c // 2])
        v_out[c] = (v_near[c] + mm(v_basis[c], local.astype(BF))).astype(BF)
        if c % 4 == 3:
            stores.append(copies.start(v_out.at[pl.ds(c - 3, 4)], out.at[pl.ds(c - 3, 4)]))
    for store in stores:
        store.wait()


def body(
    charges, leaf_basis, near_blocks, near_cols, coupling_fine, coupling_middle, coupling_coarse,
    far_cols_fine, far_cols_middle, far_cols_coarse, transfer_fine, transfer_middle, transfer_coarse,
    top_coupling, top_cols,
):
    v = pltpu.VMEM
    unit = shape((11, 64, 512))
    edge0, inner0 = kernel_call(
        pack_kernel,
        (),
        (),
        given=(charges, leaf_basis, coupling_fine, coupling_middle, coupling_coarse, top_coupling),
        outs=(unit, unit),
        limit=60,
        scratch=[
            v((11, 64, 512), BF), v((11, 64, 512), BF), v((16, 64, 64), BF), v((16, 1, 64, 64), F32),
            v((8, 1, 64, 64), F32), v((4, 1, 64, 64), F32), v((2, 2, 64, 64), F32),
        ],
    )
    edge1, edge2 = over_lvl(edge0, 1), over_lvl(edge0, -1)
    part = shape((144, PART))
    part0, part1, part2, part3 = kernel_call(
        root_kernel,
        (far_cols_fine.reshape(16), far_cols_middle.reshape(8), far_cols_coarse.reshape(4), top_cols),
        (edge0, inner0),
        (part,) * 4,
        given=(transfer_fine, transfer_middle, transfer_coarse),
        limit=60,
        scratch=[
            v((11, 64, 512), BF), v((7, 64, 512), BF), v((16, 64, 64), F32), v((8, 64, 64), F32), v((4, 64, 64), F32),
            v((LV, 144, PART), BF),
        ],
    )
    up_p, far_p, down_p = over_lvl(part1, 1), over_lvl(part2, 2), over_lvl(part3, 3)
    parts = (part0, up_p, down_p, far_p)
    root = sum(p[0:128].astype(F32) for p in parts).astype(BF).reshape(2, RANK, PART)

    edge3 = over_lvl(edge1, 1)
    late = after(inner0, up_p, down_p, far_p)
    inner2, inner1 = over_lvl(late, -1), over_lvl(late, 1)
    inner3 = over_lvl(inner2, -1)

    root = after(root, edge1, edge2)
    below, above = over_leaf(root, dz=1), over_leaf(root, dz=-1)
    three = jnp.concatenate([below, root, above], axis=0)
    far_below, far_above = over_leaf(three, dz=3), over_leaf(three[0:4], dz=-3)
    column = joined(far_below, three, far_above)
    column = after(column, inner2, edge3)
    left, right = over_leaf(column, dx=1), over_leaf(column, dx=-1)
    to_core, to_chip = kernel_call(
        ends_kernel,
        (),
        (edge0, edge1, edge2, after(edge3, left, right)),
        (shape((24, 64, 512)),) * 2,
        scratch=[v((24, 64, 512), BF)] * 2,
    )
    core_ends, chip_ends = core_swap(to_core), chip_swap(to_chip)
    across_a, across_b = over_leaf(left[0:8], dx=1), over_leaf(right[8:16], dx=-1)

    pairs = (edge0, inner0, edge1, inner1, edge2, inner2, edge3, inner3)
    fine_m, middle_m, coarse_m, to_right, to_left = kernel_call(
        moments_kernel,
        (),
        pairs,
        given=(transfer_fine, transfer_middle),
        outs=(shape((16, 64, 512)), shape((8, 64, 512)), shape((4, 64, 512))) + (shape((17, 64, 512)),) * 2,
        scratch=[
            v((LV, 11, 64, 512), BF), v((LV, 7, 64, 512), BF), v((16, 64, 64), F32), v((8, 64, 64), F32),
            v((28, 64, 512), BF),
        ],
    )
    low_m, high_m = over_leaf(to_right, step=1), over_leaf(to_left, step=-1)

    plane = joined(column, left, right, after(across_a, fine_m, core_ends, chip_ends), across_b)
    partner = core_swap(plane)
    inners = (inner0, inner1, inner2, inner3)
    term_top, columns = kernel_call(
        top_kernel,
        (),
        parts + inners + (plane, partner),
        (shape((2, 64, PART)), shape((LV, 8, PART), jnp.int32)),
        scratch=columns_scratch() + [v((LV, 64, 256), BF), v((16, 64, PART), BF), v((2, 64, PART), BF)],
    )
    up_t, down_t, far_t = over_lvl(term_top, 1), over_lvl(term_top, -1), over_lvl(term_top, 2)

    near = kernel_call(
        near_kernel,
        (near_cols,),
        pairs + (core_ends, chip_ends),
        shape((16, 64, 512), F32),
        given=(near_blocks,),
        limit=24,
        scratch=[
            v((27, 256, 512), BF), v((16, 12, 64, 256), BF), v((16, 64, 512), F32), pltpu.SMEM((16, 12), jnp.int32),
        ],
    )
    return kernel_call(
        last_kernel,
        (columns[:, 0, 0:32],),
        (fine_m, middle_m, coarse_m, low_m, high_m) + inners + (term_top, up_t, down_t, far_t, near),
        shape((16, 64, 512)),
        given=(transfer_fine, transfer_middle, transfer_coarse, leaf_basis),
        copies=40,
        scratch=[
            v((62, 64, 512), BF), v((LV, 4, 64, 512), BF), v((LV, 2, 64, PART), BF), v((16, 64, 64), F32),
            v((8, 64, 64), F32), v((4, 64, 64), F32), v((16, 64, 64), BF), v((16, 64, 512), F32), v((16, 64, 512), BF),
        ],
    )


def solution(mesh):
    placed = (
        P("leaf", "lvl", None),
        P("leaf", "lvl", None),
        P("leaf", None, "lvl", None),
        P("leaf", None),
        P("leaf", "lvl", None, None),
        P("leaf", "lvl", None, None),
        P("leaf", "lvl", None, None),
        P("leaf", "lvl"),
        P("leaf", "lvl"),
        P("leaf", "lvl"),
        P("leaf", None, None),
        P("leaf", None, None),
        P("leaf", None, None),
        P("leaf", "lvl", None, None),
        P("leaf", "lvl"),
    )
    return jax.shard_map(
        body, mesh=mesh, in_specs=placed, out_specs=P("leaf", "lvl", None), check_vma=False
    )
```

```python
import jax
import jax.numpy as jnp
from jax import lax
from jax.experimental import pallas as pl
from jax.experimental.pallas import tpu as pltpu
from jax.sharding import PartitionSpec as P

MIB = 1 << 20
BF = jnp.bfloat16
F32 = jnp.float32
ZS, XS, CS, LV = 8, 4, 2, 4
LEAVES, POINTS, VECTORS, RANK = 16, 64, 512, 64
PART = VECTORS // LV
LOW, HIGH = 6, 5
RELATIVE = (0, -1, 1, 2)


def shape(dims, dtype=BF):
    return jax.ShapeDtypeStruct(dims, dtype)


def mm(a, b):
    return jnp.dot(a, b, preferred_element_type=F32)


def leaf_pairs(dz=0, dx=0, dcore=0, step=0):
    pairs = []
    for at in range(ZS * XS * CS):
        z, x, core = at // (XS * CS), at // CS % XS, at % CS
        to = (((z + dz) % ZS) * XS + (x + dx) % XS) * CS + (core + dcore) % CS
        pairs.append((at, (to + step) % (ZS * XS * CS)))
    return pairs


def over_leaf(array, **move):
    return lax.ppermute(array, "leaf", leaf_pairs(**move))


def over_lvl(array, step):
    return lax.ppermute(array, "lvl", [(i, (i + step) % LV) for i in range(LV)])


SMEM = pl.BlockSpec(memory_space=pltpu.SMEM)
ANY = pl.BlockSpec(memory_space=pl.ANY)
HBM = pl.BlockSpec(memory_space=pltpu.HBM)


def after(array, *others):
    return lax.optimization_barrier((array,) + others)[0]


def kernel_call(kernel, scalars, arrays, outs, scratch=(), copies=32, limit=16, given=(), flops=10**6):
    return pl.pallas_call(
        kernel,
        out_shape=outs,
        in_specs=[SMEM] * len(scalars) + [ANY] * len(arrays) + [HBM] * len(given),
        out_specs=jax.tree.map(lambda _: ANY, outs),
        scratch_shapes=list(scratch) + [pltpu.SemaphoreType.DMA((copies,))],
        cost_estimate=pl.CostEstimate(flops=flops, bytes_accessed=10**5, transcendentals=0),
        compiler_params=pltpu.CompilerParams(vmem_limit_bytes=limit * MIB),
    )(*scalars, *arrays, *given)


class Copies:
    def __init__(self, sems):
        self.sems, self.count = sems, 0

    def start(self, source, target):
        copy = pltpu.make_async_copy(source, target, self.sems.at[self.count])
        self.count += 1
        copy.start()
        return copy


    def either(self, first, sources, target):
        at = self.sems.at[self.count]
        self.count += 1
        pl.when(first)(lambda: pltpu.make_async_copy(sources[0], target, at).start())
        pl.when(jnp.logical_not(first))(lambda: pltpu.make_async_copy(sources[1], target, at).start())
        return pltpu.make_async_copy(sources[0], target, at)


def lanes_of(k):
    return slice(RANK * (k % 8), RANK * (k % 8 + 1))


def own_core():
    return lax.rem(lax.axis_index("leaf"), CS)


def lvl_at(k):
    return lax.rem(lax.axis_index("lvl") + RELATIVE[k] + LV, LV)


def lifted(transfer, moments, count):
    parents = []
    for q in range(count // 2):
        both = transfer[2 * q : 2 * q + 2].reshape(2 * RANK, RANK).astype(BF).T
        parents.append(mm(both, jnp.concatenate(moments[2 * q : 2 * q + 2], axis=0)).astype(BF))
    return parents


def pack_kernel(
    charges, basis, fine_c, middle_c, coarse_c, top_c, edge, inner,
    v_edge, v_inner, v_basis, v_fine, v_middle, v_coarse, v_top, sems,
):
    copies = Copies(sems)
    edges = [
        copies.start(charges.at[pl.ds(0, 5)], v_edge.at[pl.ds(0, 5)]),
        copies.start(charges.at[pl.ds(10, 6)], v_edge.at[pl.ds(5, 6)]),
    ]
    loads = [copies.start(basis, v_basis), copies.start(charges.at[pl.ds(5, 5)], v_inner.at[pl.ds(0, 5)])]
    loads += [copies.start(a, b) for a, b in ((fine_c, v_fine), (middle_c, v_middle), (coarse_c, v_coarse), (top_c, v_top))]
    for load in edges:
        load.wait()
    out = [copies.start(v_edge, edge)]
    for load in loads:
        load.wait()
    for c in range(LEAVES):
        v_inner[5 + c // 8, :, lanes_of(c)] = v_basis[c].T
    blocks = [v_fine[c, 0] for c in range(16)] + [v_middle[c, 0] for c in range(8)]
    blocks += [v_coarse[c, 0] for c in range(4)] + [v_top[i, s] for i in range(2) for s in range(2)]
    for at, block in enumerate(blocks):
        v_inner[7 + at // 8, :, lanes_of(at)] = block.astype(BF)
    out.append(copies.start(v_inner, inner))
    for copy in out:
        copy.wait()


def leaf_of(edge, inner, c):
    if c < 5:
        return edge[c]
    return inner[c - 5] if c < 10 else edge[c - 5]


def basis_of(inner, c):
    return inner[5 + c // 8, :, lanes_of(c)]


def root_kernel(
    fine_cols, middle_cols, coarse_cols, top_cols, edge, inner, fine_t, middle_t, coarse_t,
    part0, part1, part2, part3, v_edge, v_inner, v_fine, v_middle, v_coarse, roots, sems,
):
    copies = Copies(sems)
    loads = [
        copies.start(a, b)
        for a, b in ((edge, v_edge), (inner.at[pl.ds(0, 7)], v_inner), (fine_t, v_fine), (middle_t, v_middle), (coarse_t, v_coarse))
    ]
    lane = lax.broadcasted_iota(jnp.int32, (16, PART), 1)
    info = jnp.zeros((16, PART), F32)
    leaf = lax.axis_index("leaf")
    at = 0
    for cols, count, total in ((fine_cols, 16, 1024), (middle_cols, 8, 512), (coarse_cols, 4, 256)):
        for c in range(count):
            away = ((cols[c] - leaf * count - c + total // 2) & (total - 1)) - total // 2
            info = jnp.where(lane == at, away.astype(F32), info)
            at += 1
    for i in range(2):
        for s in range(2):
            info = jnp.where(lane == at, top_cols[i, s].astype(F32), info)
            at += 1
    for load in loads:
        load.wait()
    moments = []
    for c in range(LEAVES):
        moments.append(mm(basis_of(v_inner, c), leaf_of(v_edge, v_inner, c)).astype(BF))
    moments = lifted(v_fine, moments, 16)
    moments = lifted(v_middle, moments, 8)
    moments = lifted(v_coarse, moments, 4)
    for j in range(LV):
        for i in range(2):
            roots[j, RANK * i : RANK * (i + 1)] = moments[i][:, PART * j : PART * (j + 1)]
        roots[j, 128:144] = info.astype(BF)
    out = [
        copies.start(roots.at[lax.rem(lax.axis_index("lvl") + k, LV)], part)
        for k, part in enumerate((part0, part1, part2, part3))
    ]
    for copy in out:
        copy.wait()


def read_columns(copies, parts, v_parts, v_cols, s_cols, columns):
    for load in [copies.start(part.at[pl.ds(128, 16)], v_parts.at[k]) for k, part in enumerate(parts)]:
        load.wait()
    for k in range(LV):
        v_cols[k] = v_parts[k].astype(F32)[0:8].astype(jnp.int32)
    copies.start(v_cols, s_cols).wait()
    return copies.start(v_cols, columns)


def columns_scratch():
    return [
        pltpu.VMEM((LV, 16, PART), BF), pltpu.VMEM((LV, 8, PART), jnp.int32), pltpu.SMEM((LV, 8, PART), jnp.int32),
    ]


def moments_kernel(
    edge0, inner0, edge1, inner1, edge2, inner2, edge3, inner3, fine_t, middle_t,
    fine_m, middle_m, coarse_m, to_right, to_left, edges, inners, v_fine, v_middle, moments, sems,
):
    copies = Copies(sems)
    loads = [copies.start(a, edges.at[k]) for k, a in enumerate((edge0, edge1, edge2, edge3))]
    loads += [copies.start(a.at[pl.ds(0, 7)], inners.at[k]) for k, a in enumerate((inner0, inner1, inner2, inner3))]
    loads += [copies.start(fine_t, v_fine), copies.start(middle_t, v_middle)]
    for load in loads:
        load.wait()
    fine = []
    for c in range(LEAVES):
        turned = [basis_of(inners.at[k], c) for k in range(LV)]
        points = [leaf_of(edges.at[k], inners.at[k], c) for k in range(LV)]
        fine.append(mm(jnp.concatenate(turned, axis=1), jnp.concatenate(points, axis=0)).astype(BF))
        moments[c] = fine[c]
    out = [
        copies.start(moments.at[pl.ds(8, 8)], to_right.at[pl.ds(0, 8)]),
        copies.start(moments.at[pl.ds(0, 8)], to_left.at[pl.ds(0, 8)]),
        copies.start(moments.at[pl.ds(0, 16)], fine_m),
    ]
    middle = lifted(v_fine, fine, 16)
    for c in range(8):
        moments[16 + c] = middle[c]
    out += [
        copies.start(moments.at[pl.ds(19, 5)], to_right.at[pl.ds(8, 5)]),
        copies.start(moments.at[pl.ds(16, 5)], to_left.at[pl.ds(8, 5)]),
        copies.start(moments.at[pl.ds(16, 8)], middle_m),
    ]
    coarse = lifted(v_middle, middle, 8)
    for c in range(4):
        moments[24 + c] = coarse[c]
    out += [copies.start(moments.at[pl.ds(24, 4)], to.at[pl.ds(13, 4)]) for to in (to_right, to_left)]
    out.append(copies.start(moments.at[pl.ds(24, 4)], coarse_m))
    for copy in out:
        copy.wait()


def ends_kernel(edge0, edge1, edge2, edge3, to_core, to_chip, v_core, v_chip, sems):
    copies = Copies(sems)
    core = own_core()
    loads = []
    for k, edge in enumerate((edge0, edge1, edge2, edge3)):
        loads.append(copies.start(edge.at[pl.ds(HIGH - HIGH * core, LOW)], v_core.at[pl.ds(LOW * k, LOW)]))
        loads.append(copies.start(edge.at[pl.ds(HIGH * core, LOW)], v_chip.at[pl.ds(LOW * k, LOW)]))
    for load in loads:
        load.wait()
    out = [copies.start(v_chip, to_chip), copies.start(v_core, to_core)]
    for copy in out:
        copy.wait()


def core_swap(array):
    return over_leaf(array, dcore=1)


def chip_swap(array):
    leaves = ZS * XS * CS
    return lax.ppermute(array, "leaf", [(i, (i + (1 if i % CS else -1)) % leaves) for i in range(leaves)])


def joined_kernel(*refs):
    copies = Copies(refs[-1])
    held, target, loads, out, at = refs[-2], refs[-3], [], [], 0
    for piece in refs[:-3]:
        loads.append((at, piece.shape[0], copies.start(piece, held.at[pl.ds(at, piece.shape[0])])))
        at += piece.shape[0]
    for at, count, load in loads:
        load.wait()
        out.append(copies.start(held.at[pl.ds(at, count)], target.at[pl.ds(at, count)]))
    for copy in out:
        copy.wait()


def joined(*pieces, flops=10**6):
    dims = (sum(piece.shape[0] for piece in pieces),) + pieces[0].shape[1:]
    return kernel_call(joined_kernel, (), pieces, shape(dims), scratch=[pltpu.VMEM(dims, BF)], flops=flops)


def near_kernel(
    near_cols, edge0, inner0, edge1, inner1, edge2, inner2, edge3, inner3, core_ends, chip_ends,
    blocks, out, points, held, total, slots, sems,
):
    copies = Copies(sems)
    block_copies = [copies.start(blocks.at[pl.ds(0, 4)], held.at[pl.ds(0, 4)])]
    even = own_core() == 0
    loads = []
    for k, (edge, inner) in enumerate(((edge0, inner0), (edge1, inner1), (edge2, inner2), (edge3, inner3))):
        row = pl.ds(pl.multiple_of(lvl_at(k) * POINTS, POINTS), POINTS)
        for source, first, count, leaf in ((edge, 0, 5, LOW), (inner, 0, 5, LOW + 5), (edge, 5, 6, LOW + 10)):
            loads.append(copies.start(source.at[pl.ds(first, count)], points.at[pl.ds(leaf, count), row, :]))
        core, chip = (end.at[pl.ds(LOW * k, LOW)] for end in (core_ends, chip_ends))
        loads.append(copies.either(even, (chip, core), points.at[pl.ds(0, LOW), row, :]))
        core, chip = (end.at[pl.ds(LOW * k, HIGH)] for end in (core_ends, chip_ends))
        loads.append(copies.either(even, (core, chip), points.at[pl.ds(LOW + 16, HIGH), row, :]))
    for g in range(1, 4):
        block_copies.append(copies.start(blocks.at[pl.ds(4 * g, 4)], held.at[pl.ds(4 * g, 4)]))
    first_leaf = lax.axis_index("leaf") * LEAVES

    def place_slots(c, carry):
        for s in range(12):
            slots[c, (near_cols[c, s] - first_leaf - c + LOW) & 1023] = s
        return carry

    lax.fori_loop(0, LEAVES, place_slots, 0)
    for load in loads:
        load.wait()
    stores = []
    for g in range(4):
        block_copies[g].wait()
        for source in range(15):
            held_by = [c for c in range(4) if 0 <= source - c < 12]
            rows = jnp.concatenate([held[4 * g + c, slots[4 * g + c, source - c]] for c in held_by], axis=0)
            product = mm(rows, points[4 * g + source])
            for i, c in enumerate(held_by):
                piece = product[POINTS * i : POINTS * (i + 1)]
                total[4 * g + c] = piece if source == c else total[4 * g + c] + piece
        stores.append(copies.start(total.at[pl.ds(4 * g, 4)], out.at[pl.ds(4 * g, 4)]))
    for store in stores:
        store.wait()


def top_kernel(
    part0, part1, part2, part3, own, up, down, far, mine, partner, out, columns,
    v_parts, v_cols, s_cols, v_couplings, sources, result, sems,
):
    copies = Copies(sems)
    loads = [
        copies.start(piece.at[pl.ds(10, 1), :, pl.ds(256, 256)], v_couplings.at[pl.ds(k, 1)])
        for k, piece in enumerate((own, up, down, far))
    ]
    store = read_columns(copies, (part0, part1, part2, part3), v_parts, v_cols, s_cols, columns)
    leaf = lax.axis_index("leaf")
    for k in range(LV):
        for j in range(4):
            root = s_cols[k, 0, 28 + j]
            there = root // 2
            hop = lax.rem(there // CS % XS - leaf // CS % XS + XS, XS)
            hop = jnp.where(hop == 3, 1, jnp.where(hop == 1, 2, jnp.where(hop == 2, 3, 0)))
            up_z = lax.rem(there // (XS * CS) - leaf // (XS * CS) + 4 + ZS, ZS)
            spot = hop * 16 + up_z * 2 + lax.rem(root, 2)
            here = lax.rem(there, CS) == lax.rem(leaf, CS)
            target = sources.at[(j // 2) * 8 + k * 2 + j % 2]
            loads.append(copies.either(here, (mine.at[spot], partner.at[spot]), target))
    for load in loads:
        load.wait()
    for i in range(2):
        lhs = jnp.concatenate([v_couplings[k, :, 128 * i : 128 * (i + 1)] for k in range(LV)], axis=1)
        rhs = jnp.concatenate([sources[8 * i + n] for n in range(8)], axis=0)
        result[i] = mm(lhs, rhs).astype(BF)
    copies.start(result, out).wait()
    store.wait()


def last_kernel(
    s_cols, fine_m, middle_m, coarse_m, low, high, inner0, inner1, inner2, inner3,
    own_t, up_t, down_t, far_t, near, fine_t, middle_t, coarse_t, basis, out,
    wide, v_couplings, top, v_fine, v_middle, v_coarse, v_basis, v_near, v_out, sems,
):
    copies = Copies(sems)
    early = []
    for k, inner in enumerate((inner0, inner1, inner2, inner3)):
        early.append(copies.start(inner.at[pl.ds(7, 4)], v_couplings.at[k]))
    early += [
        copies.start(coarse_t, v_coarse), copies.start(low.at[pl.ds(13, 4)], wide.at[pl.ds(0, 4)]),
        copies.start(coarse_m, wide.at[pl.ds(4, 4)]), copies.start(high.at[pl.ds(13, 4)], wide.at[pl.ds(8, 4)]),
    ]
    for k, piece in enumerate((own_t, up_t, down_t, far_t)):
        early.append(copies.start(piece, top.at[lvl_at(k)]))
    early_middle = [
        copies.start(middle_t, v_middle), copies.start(low.at[pl.ds(8, 5)], wide.at[pl.ds(12, 5)]),
        copies.start(middle_m, wide.at[pl.ds(17, 8)]), copies.start(high.at[pl.ds(8, 5)], wide.at[pl.ds(25, 5)]),
    ]
    early_fine = [
        copies.start(fine_t, v_fine), copies.start(basis, v_basis), copies.start(low.at[pl.ds(0, 8)], wide.at[pl.ds(30, 8)]),
        copies.start(fine_m, wide.at[pl.ds(38, 16)]), copies.start(high.at[pl.ds(0, 8)], wide.at[pl.ds(54, 8)]),
    ]
    near_loads = [copies.start(near.at[pl.ds(4 * g, 4)], v_near.at[pl.ds(4 * g, 4)]) for g in range(4)]

    def term(place, c, at):
        lhs = jnp.concatenate([v_couplings[k, at // 8, :, lanes_of(at)] for k in range(LV)], axis=1)
        return mm(lhs, jnp.concatenate([wide[place + c + s_cols[k, at]] for k in range(LV)], axis=0))

    for load in early:
        load.wait()
    coarse = []
    for c in range(4):
        parent = jnp.concatenate([top[j, c // 2] for j in range(LV)], axis=1)
        coarse.append((term(4, c, 24 + c) + mm(v_coarse[c].astype(BF), parent)).astype(BF))
    for load in early_middle:
        load.wait()
    middle = [
        (term(17, c, 16 + c) + mm(v_middle[c].astype(BF), coarse[c // 2])).astype(BF) for c in range(8)
    ]
    for load in early_fine:
        load.wait()
    stores = []
    for c in range(16):
        if c % 4 == 0:
            near_loads[c // 4].wait()
        local = term(38, c, c) + mm(v_fine[c].astype(BF), middle[c // 2])
        v_out[c] = (v_near[c] + mm(v_basis[c], local.astype(BF))).astype(BF)
        if c % 4 == 3:
            stores.append(copies.start(v_out.at[pl.ds(c - 3, 4)], out.at[pl.ds(c - 3, 4)]))
    for store in stores:
        store.wait()


def body(
    charges, leaf_basis, near_blocks, near_cols, coupling_fine, coupling_middle, coupling_coarse,
    far_cols_fine, far_cols_middle, far_cols_coarse, transfer_fine, transfer_middle, transfer_coarse,
    top_coupling, top_cols,
):
    v = pltpu.VMEM
    unit = shape((11, 64, 512))
    edge0, inner0 = kernel_call(
        pack_kernel,
        (),
        (),
        given=(charges, leaf_basis, coupling_fine, coupling_middle, coupling_coarse, top_coupling),
        outs=(unit, unit),
        limit=60,
        scratch=[
            v((11, 64, 512), BF), v((11, 64, 512), BF), v((16, 64, 64), BF), v((16, 1, 64, 64), F32),
            v((8, 1, 64, 64), F32), v((4, 1, 64, 64), F32), v((2, 2, 64, 64), F32),
        ],
    )
    edge1, edge2 = over_lvl(edge0, 1), over_lvl(edge0, -1)
    part = shape((144, PART))
    part0, part1, part2, part3 = kernel_call(
        root_kernel,
        (far_cols_fine.reshape(16), far_cols_middle.reshape(8), far_cols_coarse.reshape(4), top_cols),
        (edge0, inner0),
        (part,) * 4,
        given=(transfer_fine, transfer_middle, transfer_coarse),
        limit=60,
        scratch=[
            v((11, 64, 512), BF), v((7, 64, 512), BF), v((16, 64, 64), F32), v((8, 64, 64), F32), v((4, 64, 64), F32),
            v((LV, 144, PART), BF),
        ],
    )
    up_p, far_p, down_p = over_lvl(part1, 1), over_lvl(part2, 2), over_lvl(part3, 3)
    parts = (part0, up_p, down_p, far_p)
    root = sum(p[0:128].astype(F32) for p in parts).astype(BF).reshape(2, RANK, PART)

    edge3 = over_lvl(edge1, 1)
    late = after(inner0, up_p, down_p, far_p)
    inner2, inner1 = over_lvl(late, -1), over_lvl(late, 1)
    inner3 = over_lvl(inner2, -1)

    root = after(root, edge1, edge2)
    below, above = over_leaf(root, dz=1), over_leaf(root, dz=-1)
    three = jnp.concatenate([below, root, above], axis=0)
    far_below, far_above = over_leaf(three, dz=3), over_leaf(three[0:4], dz=-3)
    column = joined(far_below, three, far_above)
    column = after(column, inner2, edge3)
    left, right = over_leaf(column, dx=1), over_leaf(column, dx=-1)
    to_core, to_chip = kernel_call(
        ends_kernel,
        (),
        (edge0, edge1, edge2, after(edge3, column)),
        (shape((24, 64, 512)),) * 2,
        scratch=[v((24, 64, 512), BF)] * 2,
    )
    chip_ends = chip_swap(to_chip)
    across_a, across_b = over_leaf(left[0:8], dx=1), over_leaf(right[8:16], dx=-1)
    core_ends = core_swap(after(to_core, across_a, across_b))

    pairs = (edge0, inner0, edge1, inner1, edge2, inner2, edge3, inner3)
    fine_m, middle_m, coarse_m, to_right, to_left = kernel_call(
        moments_kernel,
        (),
        pairs,
        given=(transfer_fine, transfer_middle),
        outs=(shape((16, 64, 512)), shape((8, 64, 512)), shape((4, 64, 512))) + (shape((17, 64, 512)),) * 2,
        scratch=[
            v((LV, 11, 64, 512), BF), v((LV, 7, 64, 512), BF), v((16, 64, 64), F32), v((8, 64, 64), F32),
            v((28, 64, 512), BF),
        ],
    )
    low_m, high_m = over_leaf(to_right, step=1), over_leaf(to_left, step=-1)

    plane = joined(column, left, right, after(across_a, fine_m), across_b)
    partner = core_swap(plane)
    inners = (inner0, inner1, inner2, inner3)
    term_top, columns = kernel_call(
        top_kernel,
        (),
        parts + inners + (plane, partner),
        (shape((2, 64, PART)), shape((LV, 8, PART), jnp.int32)),
        scratch=columns_scratch() + [v((LV, 64, 256), BF), v((16, 64, PART), BF), v((2, 64, PART), BF)],
    )
    up_t, down_t, far_t = over_lvl(term_top, 1), over_lvl(term_top, -1), over_lvl(term_top, 2)

    near = kernel_call(
        near_kernel,
        (near_cols,),
        pairs + (core_ends, chip_ends),
        shape((16, 64, 512), F32),
        given=(near_blocks,),
        limit=24,
        scratch=[
            v((27, 256, 512), BF), v((16, 12, 64, 256), BF), v((16, 64, 512), F32), pltpu.SMEM((16, 12), jnp.int32),
        ],
    )
    return kernel_call(
        last_kernel,
        (columns[:, 0, 0:32],),
        (fine_m, middle_m, coarse_m, low_m, high_m) + inners + (term_top, up_t, down_t, far_t, near),
        shape((16, 64, 512)),
        given=(transfer_fine, transfer_middle, transfer_coarse, leaf_basis),
        copies=40,
        scratch=[
            v((62, 64, 512), BF), v((LV, 4, 64, 512), BF), v((LV, 2, 64, PART), BF), v((16, 64, 64), F32),
            v((8, 64, 64), F32), v((4, 64, 64), F32), v((16, 64, 64), BF), v((16, 64, 512), F32), v((16, 64, 512), BF),
        ],
    )


def solution(mesh):
    placed = (
        P("leaf", "lvl", None),
        P("leaf", "lvl", None),
        P("leaf", None, "lvl", None),
        P("leaf", None),
        P("leaf", "lvl", None, None),
        P("leaf", "lvl", None, None),
        P("leaf", "lvl", None, None),
        P("leaf", "lvl"),
        P("leaf", "lvl"),
        P("leaf", "lvl"),
        P("leaf", None, None),
        P("leaf", None, None),
        P("leaf", None, None),
        P("leaf", "lvl", None, None),
        P("leaf", "lvl"),
    )
    return jax.shard_map(
        body, mesh=mesh, in_specs=placed, out_specs=P("leaf", "lvl", None), check_vma=False
    )
```

```python
import jax
import jax.numpy as jnp
from jax import lax
from jax.experimental import pallas as pl
from jax.experimental.pallas import tpu as pltpu
from jax.sharding import PartitionSpec as P

MIB = 1 << 20
BF = jnp.bfloat16
F32 = jnp.float32
ZS, XS, CS, LV = 8, 4, 2, 4
LEAVES, POINTS, VECTORS, RANK = 16, 64, 512, 64
PART = VECTORS // LV
LOW, HIGH = 6, 5
RELATIVE = (0, -1, 1, 2)


def shape(dims, dtype=BF):
    return jax.ShapeDtypeStruct(dims, dtype)


def mm(a, b):
    return jnp.dot(a, b, preferred_element_type=F32)


def leaf_pairs(dz=0, dx=0, dcore=0, step=0):
    pairs = []
    for at in range(ZS * XS * CS):
        z, x, core = at // (XS * CS), at // CS % XS, at % CS
        to = (((z + dz) % ZS) * XS + (x + dx) % XS) * CS + (core + dcore) % CS
        pairs.append((at, (to + step) % (ZS * XS * CS)))
    return pairs


def over_leaf(array, **move):
    return lax.ppermute(array, "leaf", leaf_pairs(**move))


def over_lvl(array, step):
    return lax.ppermute(array, "lvl", [(i, (i + step) % LV) for i in range(LV)])


SMEM = pl.BlockSpec(memory_space=pltpu.SMEM)
ANY = pl.BlockSpec(memory_space=pl.ANY)
HBM = pl.BlockSpec(memory_space=pltpu.HBM)
VMEM = pl.BlockSpec(memory_space=pltpu.VMEM)


def after(array, *others):
    return lax.optimization_barrier((array,) + others)[0]


def kernel_call(kernel, scalars, arrays, outs, scratch=(), copies=32, limit=16, given=(), near=(), out_spec=ANY, flops=10**6):
    return pl.pallas_call(
        kernel,
        out_shape=outs,
        in_specs=[SMEM] * len(scalars) + [ANY] * len(arrays) + [HBM] * len(given) + [VMEM] * len(near),
        out_specs=jax.tree.map(lambda _: out_spec, outs),
        scratch_shapes=list(scratch) + [pltpu.SemaphoreType.DMA((copies,))],
        cost_estimate=pl.CostEstimate(flops=flops, bytes_accessed=10**5, transcendentals=0),
        compiler_params=pltpu.CompilerParams(vmem_limit_bytes=limit * MIB),
    )(*scalars, *arrays, *given, *near)


class Copies:
    def __init__(self, sems):
        self.sems, self.count = sems, 0

    def start(self, source, target):
        copy = pltpu.make_async_copy(source, target, self.sems.at[self.count])
        self.count += 1
        copy.start()
        return copy


    def either(self, first, sources, target):
        at = self.sems.at[self.count]
        self.count += 1
        pl.when(first)(lambda: pltpu.make_async_copy(sources[0], target, at).start())
        pl.when(jnp.logical_not(first))(lambda: pltpu.make_async_copy(sources[1], target, at).start())
        return pltpu.make_async_copy(sources[0], target, at)


def lanes_of(k):
    return slice(RANK * (k % 8), RANK * (k % 8 + 1))


def own_core():
    return lax.rem(lax.axis_index("leaf"), CS)


def lvl_at(k):
    return lax.rem(lax.axis_index("lvl") + RELATIVE[k] + LV, LV)


def lifted(transfer, moments, count):
    parents = []
    for q in range(count // 2):
        both = transfer[2 * q : 2 * q + 2].reshape(2 * RANK, RANK).astype(BF).T
        parents.append(mm(both, jnp.concatenate(moments[2 * q : 2 * q + 2], axis=0)).astype(BF))
    return parents


def pack_kernel(
    charges, basis, fine_c, middle_c, coarse_c, top_c, edge, inner,
    v_edge, v_inner, v_basis, v_fine, v_middle, v_coarse, v_top, sems,
):
    copies = Copies(sems)
    edges = [
        copies.start(charges.at[pl.ds(0, 5)], v_edge.at[pl.ds(0, 5)]),
        copies.start(charges.at[pl.ds(10, 6)], v_edge.at[pl.ds(5, 6)]),
    ]
    loads = [copies.start(basis, v_basis), copies.start(charges.at[pl.ds(5, 5)], v_inner.at[pl.ds(0, 5)])]
    loads += [copies.start(a, b) for a, b in ((fine_c, v_fine), (middle_c, v_middle), (coarse_c, v_coarse), (top_c, v_top))]
    for load in edges:
        load.wait()
    out = [copies.start(v_edge, edge)]
    for load in loads:
        load.wait()
    for c in range(LEAVES):
        v_inner[5 + c // 8, :, lanes_of(c)] = v_basis[c].T
    blocks = [v_fine[c, 0] for c in range(16)] + [v_middle[c, 0] for c in range(8)]
    blocks += [v_coarse[c, 0] for c in range(4)] + [v_top[i, s] for i in range(2) for s in range(2)]
    for at, block in enumerate(blocks):
        v_inner[7 + at // 8, :, lanes_of(at)] = block.astype(BF)
    out.append(copies.start(v_inner, inner))
    for copy in out:
        copy.wait()


def leaf_of(edge, inner, c):
    if c < 5:
        return edge[c]
    return inner[c - 5] if c < 10 else edge[c - 5]


def basis_of(inner, c):
    return inner[5 + c // 8, :, lanes_of(c)]


def root_kernel(
    fine_cols, middle_cols, coarse_cols, top_cols, edge, inner, fine_t, middle_t, coarse_t,
    part0, part1, part2, part3, v_edge, v_inner, v_fine, v_middle, v_coarse, roots, sems,
):
    copies = Copies(sems)
    loads = [
        copies.start(a, b)
        for a, b in ((edge, v_edge), (inner.at[pl.ds(0, 7)], v_inner), (fine_t, v_fine), (middle_t, v_middle), (coarse_t, v_coarse))
    ]
    lane = lax.broadcasted_iota(jnp.int32, (16, PART), 1)
    info = jnp.zeros((16, PART), F32)
    leaf = lax.axis_index("leaf")
    at = 0
    for cols, count, total in ((fine_cols, 16, 1024), (middle_cols, 8, 512), (coarse_cols, 4, 256)):
        for c in range(count):
            away = ((cols[c] - leaf * count - c + total // 2) & (total - 1)) - total // 2
            info = jnp.where(lane == at, away.astype(F32), info)
            at += 1
    for i in range(2):
        for s in range(2):
            info = jnp.where(lane == at, top_cols[i, s].astype(F32), info)
            at += 1
    for load in loads:
        load.wait()
    moments = []
    for c in range(LEAVES):
        moments.append(mm(basis_of(v_inner, c), leaf_of(v_edge, v_inner, c)).astype(BF))
    moments = lifted(v_fine, moments, 16)
    moments = lifted(v_middle, moments, 8)
    moments = lifted(v_coarse, moments, 4)
    for j in range(LV):
        for i in range(2):
            roots[j, RANK * i : RANK * (i + 1)] = moments[i][:, PART * j : PART * (j + 1)]
        roots[j, 128:144] = info.astype(BF)
    out = [
        copies.start(roots.at[lax.rem(lax.axis_index("lvl") + k, LV)], part)
        for k, part in enumerate((part0, part1, part2, part3))
    ]
    for copy in out:
        copy.wait()


def read_columns(copies, parts, v_parts, v_cols, s_cols, columns):
    for load in [copies.start(part.at[pl.ds(128, 16)], v_parts.at[k]) for k, part in enumerate(parts)]:
        load.wait()
    for k in range(LV):
        v_cols[k] = v_parts[k].astype(F32)[0:8].astype(jnp.int32)
    copies.start(v_cols, s_cols).wait()
    return copies.start(v_cols, columns)


def columns_scratch():
    return [
        pltpu.VMEM((LV, 16, PART), BF), pltpu.VMEM((LV, 8, PART), jnp.int32), pltpu.SMEM((LV, 8, PART), jnp.int32),
    ]


def moments_kernel(
    edge0, inner0, edge1, inner1, edge2, inner2, edge3, inner3, fine_t, middle_t,
    fine_m, middle_m, coarse_m, to_right, to_left, sems,
):
    edges, inners = (edge0, edge1, edge2, edge3), (inner0, inner1, inner2, inner3)
    fine = []
    for c in range(LEAVES):
        turned = [basis_of(inner, c) for inner in inners]
        points = [leaf_of(edge, inner, c) for edge, inner in zip(edges, inners, strict=True)]
        fine.append(mm(jnp.concatenate(turned, axis=1), jnp.concatenate(points, axis=0)).astype(BF))
        fine_m[c] = fine[c]
        if c < 8:
            to_left[c] = fine[c]
        else:
            to_right[c - 8] = fine[c]
    middle = lifted(fine_t, fine, 16)
    for c in range(8):
        middle_m[c] = middle[c]
        if c < 5:
            to_left[8 + c] = middle[c]
        if c >= 3:
            to_right[5 + c] = middle[c]
    coarse = lifted(middle_t, middle, 8)
    for c in range(4):
        coarse_m[c] = coarse[c]
        to_right[13 + c] = coarse[c]
        to_left[13 + c] = coarse[c]


def ends_kernel(edge0, edge1, edge2, edge3, to_core, to_chip, v_core, v_chip, sems):
    copies = Copies(sems)
    core = own_core()
    loads = []
    for k, edge in enumerate((edge0, edge1, edge2, edge3)):
        loads.append(copies.start(edge.at[pl.ds(HIGH - HIGH * core, LOW)], v_core.at[pl.ds(LOW * k, LOW)]))
        loads.append(copies.start(edge.at[pl.ds(HIGH * core, LOW)], v_chip.at[pl.ds(LOW * k, LOW)]))
    for load in loads:
        load.wait()
    out = [copies.start(v_chip, to_chip), copies.start(v_core, to_core)]
    for copy in out:
        copy.wait()


def core_swap(array):
    return over_leaf(array, dcore=1)


def chip_swap(array):
    leaves = ZS * XS * CS
    return lax.ppermute(array, "leaf", [(i, (i + (1 if i % CS else -1)) % leaves) for i in range(leaves)])


def joined_kernel(*refs):
    copies = Copies(refs[-1])
    held, target, loads, out, at = refs[-2], refs[-3], [], [], 0
    for piece in refs[:-3]:
        loads.append((at, piece.shape[0], copies.start(piece, held.at[pl.ds(at, piece.shape[0])])))
        at += piece.shape[0]
    for at, count, load in loads:
        load.wait()
        out.append(copies.start(held.at[pl.ds(at, count)], target.at[pl.ds(at, count)]))
    for copy in out:
        copy.wait()


def joined(*pieces, flops=10**6):
    dims = (sum(piece.shape[0] for piece in pieces),) + pieces[0].shape[1:]
    return kernel_call(joined_kernel, (), pieces, shape(dims), scratch=[pltpu.VMEM(dims, BF)], flops=flops)


def near_kernel(
    near_cols, edge0, inner0, edge1, inner1, edge2, inner2, edge3, inner3, core_ends, chip_ends,
    held, out, points, total, slots, sems,
):
    copies = Copies(sems)
    even = own_core() == 0
    loads = []
    for k, (edge, inner) in enumerate(((edge0, inner0), (edge1, inner1), (edge2, inner2), (edge3, inner3))):
        row = pl.ds(pl.multiple_of(lvl_at(k) * POINTS, POINTS), POINTS)
        for source, first, count, leaf in ((edge, 0, 5, LOW), (inner, 0, 5, LOW + 5), (edge, 5, 6, LOW + 10)):
            loads.append(copies.start(source.at[pl.ds(first, count)], points.at[pl.ds(leaf, count), row, :]))
        core, chip = (end.at[pl.ds(LOW * k, LOW)] for end in (core_ends, chip_ends))
        loads.append(copies.either(even, (chip, core), points.at[pl.ds(0, LOW), row, :]))
        core, chip = (end.at[pl.ds(LOW * k, HIGH)] for end in (core_ends, chip_ends))
        loads.append(copies.either(even, (core, chip), points.at[pl.ds(LOW + 16, HIGH), row, :]))
    first_leaf = lax.axis_index("leaf") * LEAVES

    def place_slots(c, carry):
        for s in range(12):
            slots[c, (near_cols[c, s] - first_leaf - c + LOW) & 1023] = s
        return carry

    lax.fori_loop(0, LEAVES, place_slots, 0)
    for load in loads:
        load.wait()
    stores = []
    for g in range(4):
        for source in range(15):
            held_by = [c for c in range(4) if 0 <= source - c < 12]
            rows = jnp.concatenate([held[4 * g + c, slots[4 * g + c, source - c]] for c in held_by], axis=0)
            product = mm(rows, points[4 * g + source])
            for i, c in enumerate(held_by):
                piece = product[POINTS * i : POINTS * (i + 1)]
                total[4 * g + c] = piece if source == c else total[4 * g + c] + piece
        stores.append(copies.start(total.at[pl.ds(4 * g, 4)], out.at[pl.ds(4 * g, 4)]))
    for store in stores:
        store.wait()


def top_kernel(
    part0, part1, part2, part3, own, up, down, far, mine, partner, out, columns,
    v_parts, v_cols, s_cols, v_couplings, sources, result, sems,
):
    copies = Copies(sems)
    loads = [
        copies.start(piece.at[pl.ds(10, 1), :, pl.ds(256, 256)], v_couplings.at[pl.ds(k, 1)])
        for k, piece in enumerate((own, up, down, far))
    ]
    store = read_columns(copies, (part0, part1, part2, part3), v_parts, v_cols, s_cols, columns)
    leaf = lax.axis_index("leaf")
    for k in range(LV):
        for j in range(4):
            root = s_cols[k, 0, 28 + j]
            there = root // 2
            hop = lax.rem(there // CS % XS - leaf // CS % XS + XS, XS)
            hop = jnp.where(hop == 3, 1, jnp.where(hop == 1, 2, jnp.where(hop == 2, 3, 0)))
            up_z = lax.rem(there // (XS * CS) - leaf // (XS * CS) + 4 + ZS, ZS)
            spot = hop * 16 + up_z * 2 + lax.rem(root, 2)
            here = lax.rem(there, CS) == lax.rem(leaf, CS)
            target = sources.at[(j // 2) * 8 + k * 2 + j % 2]
            loads.append(copies.either(here, (mine.at[spot], partner.at[spot]), target))
    for load in loads:
        load.wait()
    for i in range(2):
        lhs = jnp.concatenate([v_couplings[k, :, 128 * i : 128 * (i + 1)] for k in range(LV)], axis=1)
        rhs = jnp.concatenate([sources[8 * i + n] for n in range(8)], axis=0)
        result[i] = mm(lhs, rhs).astype(BF)
    copies.start(result, out).wait()
    store.wait()


def last_kernel(
    s_cols, fine_m, middle_m, coarse_m, low, high, inner0, inner1, inner2, inner3,
    own_t, up_t, down_t, far_t, near, fine_t, middle_t, coarse_t, basis, out, wide, top, v_out, sems,
):
    copies = Copies(sems)
    inners = (inner0, inner1, inner2, inner3)
    early = [
        copies.start(low.at[pl.ds(13, 4)], wide.at[pl.ds(0, 4)]),
        copies.start(coarse_m, wide.at[pl.ds(4, 4)]), copies.start(high.at[pl.ds(13, 4)], wide.at[pl.ds(8, 4)]),
    ]
    for k, piece in enumerate((own_t, up_t, down_t, far_t)):
        top[lvl_at(k)] = piece[...]
    early_middle = [
        copies.start(low.at[pl.ds(8, 5)], wide.at[pl.ds(12, 5)]),
        copies.start(middle_m, wide.at[pl.ds(17, 8)]), copies.start(high.at[pl.ds(8, 5)], wide.at[pl.ds(25, 5)]),
    ]
    early_fine = [
        copies.start(low.at[pl.ds(0, 8)], wide.at[pl.ds(30, 8)]),
        copies.start(fine_m, wide.at[pl.ds(38, 16)]), copies.start(high.at[pl.ds(0, 8)], wide.at[pl.ds(54, 8)]),
    ]

    def term(place, c, at):
        lhs = jnp.concatenate([inner[7 + at // 8, :, lanes_of(at)] for inner in inners], axis=1)
        return mm(lhs, jnp.concatenate([wide[place + c + s_cols[k, at]] for k in range(LV)], axis=0))

    for load in early:
        load.wait()
    coarse = []
    for c in range(4):
        parent = jnp.concatenate([top[j, c // 2] for j in range(LV)], axis=1)
        coarse.append((term(4, c, 24 + c) + mm(coarse_t[c].astype(BF), parent)).astype(BF))
    for load in early_middle:
        load.wait()
    middle = [
        (term(17, c, 16 + c) + mm(middle_t[c].astype(BF), coarse[c // 2])).astype(BF) for c in range(8)
    ]
    for load in early_fine:
        load.wait()
    stores = []
    for c in range(16):
        local = term(38, c, c) + mm(fine_t[c].astype(BF), middle[c // 2])
        v_out[c] = (near[c] + mm(basis[c], local.astype(BF))).astype(BF)
        if c % 4 == 3:
            stores.append(copies.start(v_out.at[pl.ds(c - 3, 4)], out.at[pl.ds(c - 3, 4)]))
    for store in stores:
        store.wait()


def body(
    charges, leaf_basis, near_blocks, near_cols, coupling_fine, coupling_middle, coupling_coarse,
    far_cols_fine, far_cols_middle, far_cols_coarse, transfer_fine, transfer_middle, transfer_coarse,
    top_coupling, top_cols,
):
    v = pltpu.VMEM
    unit = shape((11, 64, 512))
    edge0, inner0 = kernel_call(
        pack_kernel,
        (),
        (),
        given=(charges, leaf_basis, coupling_fine, coupling_middle, coupling_coarse, top_coupling),
        outs=(unit, unit),
        limit=60,
        scratch=[
            v((11, 64, 512), BF), v((11, 64, 512), BF), v((16, 64, 64), BF), v((16, 1, 64, 64), F32),
            v((8, 1, 64, 64), F32), v((4, 1, 64, 64), F32), v((2, 2, 64, 64), F32),
        ],
    )
    edge1, edge2 = over_lvl(edge0, 1), over_lvl(edge0, -1)
    part = shape((144, PART))
    part0, part1, part2, part3 = kernel_call(
        root_kernel,
        (far_cols_fine.reshape(16), far_cols_middle.reshape(8), far_cols_coarse.reshape(4), top_cols),
        (edge0, inner0),
        (part,) * 4,
        given=(transfer_fine, transfer_middle, transfer_coarse),
        limit=60,
        scratch=[
            v((11, 64, 512), BF), v((7, 64, 512), BF), v((16, 64, 64), F32), v((8, 64, 64), F32), v((4, 64, 64), F32),
            v((LV, 144, PART), BF),
        ],
    )
    up_p, far_p, down_p = over_lvl(part1, 1), over_lvl(part2, 2), over_lvl(part3, 3)
    parts = (part0, up_p, down_p, far_p)
    root = sum(p[0:128].astype(F32) for p in parts).astype(BF).reshape(2, RANK, PART)

    edge3 = over_lvl(edge1, 1)
    late = after(inner0, up_p, down_p, far_p)
    inner2, inner1 = over_lvl(late, -1), over_lvl(late, 1)
    inner3 = over_lvl(inner2, -1)

    root = after(root, edge1, edge2)
    below, above = over_leaf(root, dz=1), over_leaf(root, dz=-1)
    three = jnp.concatenate([below, root, above], axis=0)
    far_below, far_above = over_leaf(three, dz=3), over_leaf(three[0:4], dz=-3)
    column = joined(far_below, three, far_above)
    column = after(column, inner2, edge3)
    left, right = over_leaf(column, dx=1), over_leaf(column, dx=-1)
    to_core, to_chip = kernel_call(
        ends_kernel,
        (),
        (edge0, edge1, edge2, after(edge3, column)),
        (shape((24, 64, 512)),) * 2,
        scratch=[v((24, 64, 512), BF)] * 2,
    )
    chip_ends = chip_swap(to_chip)
    across_a, across_b = over_leaf(left[0:8], dx=1), over_leaf(right[8:16], dx=-1)
    core_ends = core_swap(after(to_core, across_a, across_b))

    pairs = (edge0, inner0, edge1, inner1, edge2, inner2, edge3, inner3)
    fine_m, middle_m, coarse_m, to_right, to_left = kernel_call(
        moments_kernel,
        (),
        (),
        near=pairs + (transfer_fine, transfer_middle),
        outs=(shape((16, 64, 512)), shape((8, 64, 512)), shape((4, 64, 512))) + (shape((17, 64, 512)),) * 2,
        out_spec=VMEM,
    )
    low_m, high_m = over_leaf(to_right, step=1), over_leaf(to_left, step=-1)

    plane = joined(column, left, right, after(across_a, fine_m), across_b)
    partner = core_swap(plane)
    inners = (inner0, inner1, inner2, inner3)
    term_top, columns = kernel_call(
        top_kernel,
        (),
        parts + inners + (plane, partner),
        (shape((2, 64, PART)), shape((LV, 8, PART), jnp.int32)),
        scratch=columns_scratch() + [v((LV, 64, 256), BF), v((16, 64, PART), BF), v((2, 64, PART), BF)],
    )
    up_t, down_t, far_t = over_lvl(term_top, 1), over_lvl(term_top, -1), over_lvl(term_top, 2)

    near = kernel_call(
        near_kernel,
        (near_cols,),
        pairs + (core_ends, chip_ends),
        shape((16, 64, 512), F32),
        near=(near_blocks,),
        limit=24,
        scratch=[
            v((27, 256, 512), BF), v((16, 64, 512), F32), pltpu.SMEM((16, 12), jnp.int32),
        ],
    )
    return kernel_call(
        last_kernel,
        (columns[:, 0, 0:32],),
        (fine_m, middle_m, coarse_m, low_m, high_m),
        shape((16, 64, 512)),
        near=inners
        + (term_top, up_t, down_t, far_t, near, transfer_fine, transfer_middle, transfer_coarse, leaf_basis),
        scratch=[v((62, 64, 512), BF), v((LV, 2, 64, PART), BF), v((16, 64, 512), BF)],
    )


def solution(mesh):
    placed = (
        P("leaf", "lvl", None),
        P("leaf", "lvl", None),
        P("leaf", None, "lvl", None),
        P("leaf", None),
        P("leaf", "lvl", None, None),
        P("leaf", "lvl", None, None),
        P("leaf", "lvl", None, None),
        P("leaf", "lvl"),
        P("leaf", "lvl"),
        P("leaf", "lvl"),
        P("leaf", None, None),
        P("leaf", None, None),
        P("leaf", None, None),
        P("leaf", "lvl", None, None),
        P("leaf", "lvl"),
    )
    return jax.shard_map(
        body, mesh=mesh, in_specs=placed, out_specs=P("leaf", "lvl", None), check_vma=False
    )
```

```python
import jax
import jax.numpy as jnp
from jax import lax
from jax.experimental import pallas as pl
from jax.experimental.pallas import tpu as pltpu
from jax.sharding import PartitionSpec as P

MIB = 1 << 20
BF = jnp.bfloat16
F32 = jnp.float32
ZS, XS, CS, LV = 8, 4, 2, 4
LEAVES, POINTS, VECTORS, RANK = 16, 64, 512, 64
PART = VECTORS // LV
LOW, HIGH = 6, 5
RELATIVE = (0, -1, 1, 2)


def shape(dims, dtype=BF):
    return jax.ShapeDtypeStruct(dims, dtype)


def mm(a, b):
    return jnp.dot(a, b, preferred_element_type=F32)


def leaf_pairs(dz=0, dx=0, dcore=0, step=0):
    pairs = []
    for at in range(ZS * XS * CS):
        z, x, core = at // (XS * CS), at // CS % XS, at % CS
        to = (((z + dz) % ZS) * XS + (x + dx) % XS) * CS + (core + dcore) % CS
        pairs.append((at, (to + step) % (ZS * XS * CS)))
    return pairs


def over_leaf(array, **move):
    return lax.ppermute(array, "leaf", leaf_pairs(**move))


def over_lvl(array, step):
    return lax.ppermute(array, "lvl", [(i, (i + step) % LV) for i in range(LV)])


SMEM = pl.BlockSpec(memory_space=pltpu.SMEM)
ANY = pl.BlockSpec(memory_space=pl.ANY)
HBM = pl.BlockSpec(memory_space=pltpu.HBM)
VMEM = pl.BlockSpec(memory_space=pltpu.VMEM)


def after(array, *others):
    return lax.optimization_barrier((array,) + others)[0]


def kernel_call(kernel, scalars, arrays, outs, scratch=(), copies=32, limit=16, given=(), near=(), out_spec=ANY, flops=10**6):
    return pl.pallas_call(
        kernel,
        out_shape=outs,
        in_specs=[SMEM] * len(scalars) + [ANY] * len(arrays) + [HBM] * len(given) + [VMEM] * len(near),
        out_specs=jax.tree.map(lambda _: out_spec, outs),
        scratch_shapes=list(scratch) + [pltpu.SemaphoreType.DMA((copies,))],
        cost_estimate=pl.CostEstimate(flops=flops, bytes_accessed=10**5, transcendentals=0),
        compiler_params=pltpu.CompilerParams(vmem_limit_bytes=limit * MIB),
    )(*scalars, *arrays, *given, *near)


class Copies:
    def __init__(self, sems):
        self.sems, self.count = sems, 0

    def start(self, source, target):
        copy = pltpu.make_async_copy(source, target, self.sems.at[self.count])
        self.count += 1
        copy.start()
        return copy


    def either(self, first, sources, target):
        at = self.sems.at[self.count]
        self.count += 1
        pl.when(first)(lambda: pltpu.make_async_copy(sources[0], target, at).start())
        pl.when(jnp.logical_not(first))(lambda: pltpu.make_async_copy(sources[1], target, at).start())
        return pltpu.make_async_copy(sources[0], target, at)


def lanes_of(k):
    return slice(RANK * (k % 8), RANK * (k % 8 + 1))


def own_core():
    return lax.rem(lax.axis_index("leaf"), CS)


def lvl_at(k):
    return lax.rem(lax.axis_index("lvl") + RELATIVE[k] + LV, LV)


def lifted(transfer, moments, count):
    parents = []
    for q in range(count // 2):
        both = transfer[2 * q : 2 * q + 2].reshape(2 * RANK, RANK).astype(BF).T
        parents.append(mm(both, jnp.concatenate(moments[2 * q : 2 * q + 2], axis=0)).astype(BF))
    return parents


def pack_kernel(
    charges, basis, fine_c, middle_c, coarse_c, top_c, edge, inner,
    v_edge, v_inner, v_basis, v_fine, v_middle, v_coarse, v_top, sems,
):
    copies = Copies(sems)
    edges = [
        copies.start(charges.at[pl.ds(0, 5)], v_edge.at[pl.ds(0, 5)]),
        copies.start(charges.at[pl.ds(10, 6)], v_edge.at[pl.ds(5, 6)]),
    ]
    loads = [copies.start(basis, v_basis), copies.start(charges.at[pl.ds(5, 5)], v_inner.at[pl.ds(0, 5)])]
    loads += [copies.start(a, b) for a, b in ((fine_c, v_fine), (middle_c, v_middle), (coarse_c, v_coarse), (top_c, v_top))]
    for load in edges:
        load.wait()
    out = [copies.start(v_edge, edge)]
    for load in loads:
        load.wait()
    for c in range(LEAVES):
        v_inner[5 + c // 8, :, lanes_of(c)] = v_basis[c].T
    blocks = [v_fine[c, 0] for c in range(16)] + [v_middle[c, 0] for c in range(8)]
    blocks += [v_coarse[c, 0] for c in range(4)] + [v_top[i, s] for i in range(2) for s in range(2)]
    for at, block in enumerate(blocks):
        v_inner[7 + at // 8, :, lanes_of(at)] = block.astype(BF)
    out.append(copies.start(v_inner, inner))
    for copy in out:
        copy.wait()


def leaf_of(edge, inner, c):
    if c < 5:
        return edge[c]
    return inner[c - 5] if c < 10 else edge[c - 5]


def basis_of(inner, c):
    return inner[5 + c // 8, :, lanes_of(c)]


def root_kernel(
    fine_cols, middle_cols, coarse_cols, top_cols, edge, inner, fine_t, middle_t, coarse_t,
    part0, part1, part2, part3, v_edge, v_inner, v_fine, v_middle, v_coarse, roots, sems,
):
    copies = Copies(sems)
    loads = [
        copies.start(a, b)
        for a, b in ((edge, v_edge), (inner.at[pl.ds(0, 7)], v_inner), (fine_t, v_fine), (middle_t, v_middle), (coarse_t, v_coarse))
    ]
    lane = lax.broadcasted_iota(jnp.int32, (16, PART), 1)
    info = jnp.zeros((16, PART), F32)
    leaf = lax.axis_index("leaf")
    at = 0
    for cols, count, total in ((fine_cols, 16, 1024), (middle_cols, 8, 512), (coarse_cols, 4, 256)):
        for c in range(count):
            away = ((cols[c] - leaf * count - c + total // 2) & (total - 1)) - total // 2
            info = jnp.where(lane == at, away.astype(F32), info)
            at += 1
    for i in range(2):
        for s in range(2):
            info = jnp.where(lane == at, top_cols[i, s].astype(F32), info)
            at += 1
    for load in loads:
        load.wait()
    moments = []
    for c in range(LEAVES):
        moments.append(mm(basis_of(v_inner, c), leaf_of(v_edge, v_inner, c)).astype(BF))
    moments = lifted(v_fine, moments, 16)
    moments = lifted(v_middle, moments, 8)
    moments = lifted(v_coarse, moments, 4)
    for j in range(LV):
        for i in range(2):
            roots[j, RANK * i : RANK * (i + 1)] = moments[i][:, PART * j : PART * (j + 1)]
        roots[j, 128:144] = info.astype(BF)
    out = [
        copies.start(roots.at[lax.rem(lax.axis_index("lvl") + k, LV)], part)
        for k, part in enumerate((part0, part1, part2, part3))
    ]
    for copy in out:
        copy.wait()


def read_columns(copies, parts, v_parts, v_cols, s_cols, columns):
    for load in [copies.start(part.at[pl.ds(128, 16)], v_parts.at[k]) for k, part in enumerate(parts)]:
        load.wait()
    for k in range(LV):
        v_cols[k] = v_parts[k].astype(F32)[0:8].astype(jnp.int32)
    copies.start(v_cols, s_cols).wait()
    return copies.start(v_cols, columns)


def columns_scratch():
    return [
        pltpu.VMEM((LV, 16, PART), BF), pltpu.VMEM((LV, 8, PART), jnp.int32), pltpu.SMEM((LV, 8, PART), jnp.int32),
    ]


def moments_kernel(
    edge0, inner0, edge1, inner1, edge2, inner2, edge3, inner3, fine_t, middle_t,
    fine_m, middle_m, coarse_m, to_right, to_left, sems,
):
    edges, inners = (edge0, edge1, edge2, edge3), (inner0, inner1, inner2, inner3)
    fine = []
    for c in range(LEAVES):
        turned = [basis_of(inner, c) for inner in inners]
        points = [leaf_of(edge, inner, c) for edge, inner in zip(edges, inners, strict=True)]
        fine.append(mm(jnp.concatenate(turned, axis=1), jnp.concatenate(points, axis=0)).astype(BF))
        fine_m[c] = fine[c]
        if c < 8:
            to_left[c] = fine[c]
        else:
            to_right[c - 8] = fine[c]
    middle = lifted(fine_t, fine, 16)
    for c in range(8):
        middle_m[c] = middle[c]
        if c < 5:
            to_left[8 + c] = middle[c]
        if c >= 3:
            to_right[5 + c] = middle[c]
    coarse = lifted(middle_t, middle, 8)
    for c in range(4):
        coarse_m[c] = coarse[c]
        to_right[13 + c] = coarse[c]
        to_left[13 + c] = coarse[c]


def ends_kernel(edge0, edge1, edge2, edge3, to_core, to_chip, v_core, v_chip, sems):
    copies = Copies(sems)
    core = own_core()
    loads = []
    for k, edge in enumerate((edge0, edge1, edge2, edge3)):
        loads.append(copies.start(edge.at[pl.ds(HIGH - HIGH * core, LOW)], v_core.at[pl.ds(LOW * k, LOW)]))
        loads.append(copies.start(edge.at[pl.ds(HIGH * core, LOW)], v_chip.at[pl.ds(LOW * k, LOW)]))
    for load in loads:
        load.wait()
    out = [copies.start(v_chip, to_chip), copies.start(v_core, to_core)]
    for copy in out:
        copy.wait()


def core_swap(array):
    return over_leaf(array, dcore=1)


def chip_swap(array):
    leaves = ZS * XS * CS
    return lax.ppermute(array, "leaf", [(i, (i + (1 if i % CS else -1)) % leaves) for i in range(leaves)])


def joined_kernel(*refs):
    copies = Copies(refs[-1])
    held, target, loads, out, at = refs[-2], refs[-3], [], [], 0
    for piece in refs[:-3]:
        loads.append((at, piece.shape[0], copies.start(piece, held.at[pl.ds(at, piece.shape[0])])))
        at += piece.shape[0]
    for at, count, load in loads:
        load.wait()
        out.append(copies.start(held.at[pl.ds(at, count)], target.at[pl.ds(at, count)]))
    for copy in out:
        copy.wait()


def joined(*pieces, flops=10**6):
    dims = (sum(piece.shape[0] for piece in pieces),) + pieces[0].shape[1:]
    return kernel_call(joined_kernel, (), pieces, shape(dims), scratch=[pltpu.VMEM(dims, BF)], flops=flops)


def near_kernel(
    near_cols, edge0, inner0, edge1, inner1, edge2, inner2, edge3, inner3, core_ends, chip_ends,
    held, out, points, total, slots, sems,
):
    copies = Copies(sems)
    even = own_core() == 0
    loads = []
    for k, (edge, inner) in enumerate(((edge0, inner0), (edge1, inner1), (edge2, inner2), (edge3, inner3))):
        row = pl.ds(pl.multiple_of(lvl_at(k) * POINTS, POINTS), POINTS)
        for source, first, count, leaf in ((edge, 0, 5, LOW), (inner, 0, 5, LOW + 5), (edge, 5, 6, LOW + 10)):
            loads.append(copies.start(source.at[pl.ds(first, count)], points.at[pl.ds(leaf, count), row, :]))
        core, chip = (end.at[pl.ds(LOW * k, LOW)] for end in (core_ends, chip_ends))
        loads.append(copies.either(even, (chip, core), points.at[pl.ds(0, LOW), row, :]))
        core, chip = (end.at[pl.ds(LOW * k, HIGH)] for end in (core_ends, chip_ends))
        loads.append(copies.either(even, (core, chip), points.at[pl.ds(LOW + 16, HIGH), row, :]))
    first_leaf = lax.axis_index("leaf") * LEAVES

    def place_slots(c, carry):
        for s in range(12):
            slots[c, (near_cols[c, s] - first_leaf - c + LOW) & 1023] = s
        return carry

    lax.fori_loop(0, LEAVES, place_slots, 0)
    for load in loads:
        load.wait()
    stores = []
    for g in range(4):
        for source in range(15):
            held_by = [c for c in range(4) if 0 <= source - c < 12]
            rows = jnp.concatenate([held[4 * g + c, slots[4 * g + c, source - c]] for c in held_by], axis=0)
            product = mm(rows, points[4 * g + source])
            for i, c in enumerate(held_by):
                piece = product[POINTS * i : POINTS * (i + 1)]
                total[4 * g + c] = piece if source == c else total[4 * g + c] + piece
        stores.append(copies.start(total.at[pl.ds(4 * g, 4)], out.at[pl.ds(4 * g, 4)]))
    for store in stores:
        store.wait()


def top_kernel(
    part0, part1, part2, part3, own, up, down, far, mine, partner, out, columns,
    v_parts, v_cols, s_cols, v_couplings, sources, result, sems,
):
    copies = Copies(sems)
    loads = [
        copies.start(piece.at[pl.ds(10, 1), :, pl.ds(256, 256)], v_couplings.at[pl.ds(k, 1)])
        for k, piece in enumerate((own, up, down, far))
    ]
    store = read_columns(copies, (part0, part1, part2, part3), v_parts, v_cols, s_cols, columns)
    leaf = lax.axis_index("leaf")
    for k in range(LV):
        for j in range(4):
            root = s_cols[k, 0, 28 + j]
            there = root // 2
            hop = lax.rem(there // CS % XS - leaf // CS % XS + XS, XS)
            hop = jnp.where(hop == 3, 1, jnp.where(hop == 1, 2, jnp.where(hop == 2, 3, 0)))
            up_z = lax.rem(there // (XS * CS) - leaf // (XS * CS) + 4 + ZS, ZS)
            spot = hop * 16 + up_z * 2 + lax.rem(root, 2)
            here = lax.rem(there, CS) == lax.rem(leaf, CS)
            target = sources.at[(j // 2) * 8 + k * 2 + j % 2]
            loads.append(copies.either(here, (mine.at[spot], partner.at[spot]), target))
    for load in loads:
        load.wait()
    for i in range(2):
        lhs = jnp.concatenate([v_couplings[k, :, 128 * i : 128 * (i + 1)] for k in range(LV)], axis=1)
        rhs = jnp.concatenate([sources[8 * i + n] for n in range(8)], axis=0)
        result[i] = mm(lhs, rhs).astype(BF)
    copies.start(result, out).wait()
    store.wait()


def last_kernel(
    s_cols, fine_m, middle_m, coarse_m, low, high, inner0, inner1, inner2, inner3,
    own_t, up_t, down_t, far_t, near, fine_t, middle_t, coarse_t, basis, out, v_couplings, top, v_out, slots, sems,
):
    copies = Copies(sems)
    loads = [
        copies.start(inner.at[pl.ds(7, 4)], v_couplings.at[k])
        for k, inner in enumerate((inner0, inner1, inner2, inner3))
    ]
    for k, piece in enumerate((own_t, up_t, down_t, far_t)):
        top[lvl_at(k)] = piece[...]
    for at in range(28):
        reach = 8 if at < 16 else 5 if at < 24 else 4
        for k in range(LV):
            away = s_cols[k, at]
            slots[at, jnp.where(away < 0, away + reach, away - reach + 3)] = k
    for load in loads:
        load.wait()

    def term(moments, first, reach, rim, c, at):
        count = moments.shape[0]
        lhs, rhs = [], []
        for place, away in enumerate((-reach, 1 - reach, reach - 1, reach)):
            lhs.append(v_couplings[slots[at, place], at // 8, :, lanes_of(at)])
            source = c + away
            if source < 0:
                rhs.append(low[first + rim + source])
            elif source < count:
                rhs.append(moments[source])
            else:
                rhs.append(high[first + source - count])
        return mm(jnp.concatenate(lhs, axis=1), jnp.concatenate(rhs, axis=0))

    coarse = []
    for c in range(4):
        parent = jnp.concatenate([top[j, c // 2] for j in range(LV)], axis=1)
        local = term(coarse_m, 13, 4, 4, c, 24 + c) + mm(coarse_t[c].astype(BF), parent)
        coarse.append(local.astype(BF))
    middle = [
        (term(middle_m, 8, 5, 5, c, 16 + c) + mm(middle_t[c].astype(BF), coarse[c // 2])).astype(BF)
        for c in range(8)
    ]
    stores = []
    for c in range(16):
        local = term(fine_m, 0, 8, 8, c, c) + mm(fine_t[c].astype(BF), middle[c // 2])
        v_out[c] = (near[c] + mm(basis[c], local.astype(BF))).astype(BF)
        if c % 4 == 3:
            stores.append(copies.start(v_out.at[pl.ds(c - 3, 4)], out.at[pl.ds(c - 3, 4)]))
    for store in stores:
        store.wait()


def body(
    charges, leaf_basis, near_blocks, near_cols, coupling_fine, coupling_middle, coupling_coarse,
    far_cols_fine, far_cols_middle, far_cols_coarse, transfer_fine, transfer_middle, transfer_coarse,
    top_coupling, top_cols,
):
    v = pltpu.VMEM
    unit = shape((11, 64, 512))
    edge0, inner0 = kernel_call(
        pack_kernel,
        (),
        (),
        given=(charges, leaf_basis, coupling_fine, coupling_middle, coupling_coarse, top_coupling),
        outs=(unit, unit),
        limit=60,
        scratch=[
            v((11, 64, 512), BF), v((11, 64, 512), BF), v((16, 64, 64), BF), v((16, 1, 64, 64), F32),
            v((8, 1, 64, 64), F32), v((4, 1, 64, 64), F32), v((2, 2, 64, 64), F32),
        ],
    )
    edge1, edge2 = over_lvl(edge0, 1), over_lvl(edge0, -1)
    part = shape((144, PART))
    part0, part1, part2, part3 = kernel_call(
        root_kernel,
        (far_cols_fine.reshape(16), far_cols_middle.reshape(8), far_cols_coarse.reshape(4), top_cols),
        (edge0, inner0),
        (part,) * 4,
        given=(transfer_fine, transfer_middle, transfer_coarse),
        limit=60,
        scratch=[
            v((11, 64, 512), BF), v((7, 64, 512), BF), v((16, 64, 64), F32), v((8, 64, 64), F32), v((4, 64, 64), F32),
            v((LV, 144, PART), BF),
        ],
    )
    up_p, far_p, down_p = over_lvl(part1, 1), over_lvl(part2, 2), over_lvl(part3, 3)
    parts = (part0, up_p, down_p, far_p)
    root = sum(p[0:128].astype(F32) for p in parts).astype(BF).reshape(2, RANK, PART)

    edge3 = over_lvl(edge1, 1)
    late = after(inner0, up_p, down_p, far_p)
    inner2, inner1 = over_lvl(late, -1), over_lvl(late, 1)
    inner3 = over_lvl(inner2, -1)

    root = after(root, edge1, edge2)
    below, above = over_leaf(root, dz=1), over_leaf(root, dz=-1)
    three = jnp.concatenate([below, root, above], axis=0)
    far_below, far_above = over_leaf(three, dz=3), over_leaf(three[0:4], dz=-3)
    column = joined(far_below, three, far_above)
    column = after(column, inner2, edge3)
    left, right = over_leaf(column, dx=1), over_leaf(column, dx=-1)
    to_core, to_chip = kernel_call(
        ends_kernel,
        (),
        (edge0, edge1, edge2, after(edge3, column)),
        (shape((24, 64, 512)),) * 2,
        scratch=[v((24, 64, 512), BF)] * 2,
    )
    chip_ends = chip_swap(to_chip)
    across_a, across_b = over_leaf(left[0:8], dx=1), over_leaf(right[8:16], dx=-1)
    core_ends = core_swap(after(to_core, across_a, across_b))

    pairs = (edge0, inner0, edge1, inner1, edge2, inner2, edge3, inner3)
    fine_m, middle_m, coarse_m, to_right, to_left = kernel_call(
        moments_kernel,
        (),
        (),
        near=pairs + (transfer_fine, transfer_middle),
        outs=(shape((16, 64, 512)), shape((8, 64, 512)), shape((4, 64, 512))) + (shape((17, 64, 512)),) * 2,
        out_spec=VMEM,
    )
    low_m, high_m = over_leaf(to_right, step=1), over_leaf(to_left, step=-1)

    plane = joined(column, left, right, after(across_a, fine_m), across_b)
    partner = core_swap(plane)
    inners = (inner0, inner1, inner2, inner3)
    term_top, columns = kernel_call(
        top_kernel,
        (),
        parts + inners + (plane, partner),
        (shape((2, 64, PART)), shape((LV, 8, PART), jnp.int32)),
        scratch=columns_scratch() + [v((LV, 64, 256), BF), v((16, 64, PART), BF), v((2, 64, PART), BF)],
    )
    up_t, down_t, far_t = over_lvl(term_top, 1), over_lvl(term_top, -1), over_lvl(term_top, 2)

    near = kernel_call(
        near_kernel,
        (near_cols,),
        pairs + (core_ends, chip_ends),
        shape((16, 64, 512), F32),
        near=(near_blocks,),
        limit=24,
        scratch=[
            v((27, 256, 512), BF), v((16, 64, 512), F32), pltpu.SMEM((16, 12), jnp.int32),
        ],
    )
    return kernel_call(
        last_kernel,
        (columns[:, 0, 0:32],),
        (),
        shape((16, 64, 512)),
        near=(fine_m, middle_m, coarse_m, low_m, high_m) + inners
        + (term_top, up_t, down_t, far_t, near, transfer_fine, transfer_middle, transfer_coarse, leaf_basis),
        scratch=[
            v((LV, 4, 64, 512), BF), v((LV, 2, 64, PART), BF), v((16, 64, 512), BF), pltpu.SMEM((28, LV), jnp.int32),
        ],
    )


def solution(mesh):
    placed = (
        P("leaf", "lvl", None),
        P("leaf", "lvl", None),
        P("leaf", None, "lvl", None),
        P("leaf", None),
        P("leaf", "lvl", None, None),
        P("leaf", "lvl", None, None),
        P("leaf", "lvl", None, None),
        P("leaf", "lvl"),
        P("leaf", "lvl"),
        P("leaf", "lvl"),
        P("leaf", None, None),
        P("leaf", None, None),
        P("leaf", None, None),
        P("leaf", "lvl", None, None),
        P("leaf", "lvl"),
    )
    return jax.shard_map(
        body, mesh=mesh, in_specs=placed, out_specs=P("leaf", "lvl", None), check_vma=False
    )
```
